128 devices in a mesh: rows: 16 (over z, x), dims: 8 (over y, core).
Axes of the slice: x: 4, y: 4, z: 4, core: 2. Of those that a mesh axis runs over, the one named last changes fastest.
Arguments:
- embeddings: bfloat16 [131072, 1024], P('rows', 'dims'), may hold values from -200 to 200
- sign_flips: int32 [1024], P('dims'), may hold values from -1 to 1, as said below
- row_order: int32 [131072], P('rows'), may hold values from 0 to 8191, as said below
- codebook: bfloat16 [64, 256, 16], replicated, may hold values from -4 to 4
Outputs:
- decoded: bfloat16 [131072, 1024], P(('rows', 'dims'))
- new_codebook: float32 [64, 256, 16], replicated
The draws below stay inside these ranges and needn't reach their ends.
Inputs may be any that keep to these rules, and one draw needn't show every extreme that they name: `sign_flips`: each entry is -1 or 1. `row_order`: within each aligned block of 8192 entries the values are a permutation of 0 to 8191.
All inputs are finite; a program needn't handle non-finite values.
Results may differ from the reference program's by a relative error of at most 0.0065.
The reference program's roundings to bfloat16 on the way (of `rotated`, `regrouped` and `weights`) count: a program that leaves them out, or rounds other values in their place, can miss the bound.
Values may be sent and summed in bfloat16 or wider, within the bound.
A program may use at most 64 MiB of HBM per device.

```python
import math
import jax
import jax.numpy as jnp
from jax import lax

D = 1024
SUBSPACES = 64
CODES = 256
ROW_DEV = 1024
SUBDIM = 16
ROWS = 131072
BLOCK = 8192
PIECE = 64


def draw_embeddings(key, part):
    key = jax.random.fold_in(key, 7)
    row_key, col_key, value_key = jax.random.split(key, 3)
    slot_position = jnp.arange(ROWS, dtype=jnp.float32) / ROWS
    column = jnp.arange(D, dtype=jnp.float32) / D
    rough = jnp.exp(jax.random.uniform(row_key, (ROWS, 1), jnp.float32, math.log(0.5), math.log(2.0)))
    ramp = 3.0 ** (0.5 * slot_position)
    values = jnp.clip(jax.random.normal(value_key, (ROWS, D), jnp.float32), -4.0, 4.0)
    spread = jnp.exp(jax.random.uniform(col_key, (1, D), jnp.float32, 0.0, math.log(2.0))) * (3.0 ** (0.5 * column))[None, :]
    return (values * rough * ramp[:, None] * spread).astype(jnp.bfloat16)


def draw_sign_flips(key, part):
    key = jax.random.fold_in(key, 3)
    return (jax.random.randint(key, (D,), 0, 2) * 2 - 1).astype(jnp.int32)


def draw_row_order(key, part):
    key = jax.random.fold_in(key, 5)
    block_keys = jax.random.split(key, ROWS // BLOCK)

    def shuffle_block(block_key):
        return jax.random.permutation(block_key, BLOCK)
    return jax.vmap(shuffle_block)(block_keys).reshape(ROWS).astype(jnp.int32)


def centred(rng, shape, scale, limit, kind=jnp.bfloat16):
    return jnp.clip(scale * jax.random.normal(rng, shape, jnp.float32), -limit, limit).astype(kind)


def setup_inputs(seed: int = 0) -> dict:
    key_of = jax.random.split(jax.random.key(seed), 5)
    return {
        "embeddings": draw_embeddings(jax.random.fold_in(key_of[4], 71), 0),
        "sign_flips": draw_sign_flips(jax.random.fold_in(key_of[4], 71), 0),
        "row_order": draw_row_order(jax.random.fold_in(key_of[4], 71), 0),
        "codebook": centred(key_of[3], (SUBSPACES, CODES, SUBDIM), 1.0, 4.0),
    }


ANISO_GAIN = 1.0
SOFTNESS_LEVEL = 4.0
PRIOR_MASS = 1.0
STABILITY_FLOOR = 1e-06

def hadamard_table(order_size, number_type):
    row_ids = jnp.arange(order_size, dtype=jnp.int32)[:, None]
    column_numbers = jnp.arange(order_size, dtype=jnp.int32)[None, :]
    shared_offset = jnp.bitwise_and(row_ids, column_numbers)
    parity = jnp.zeros((order_size, order_size), jnp.int32)
    for shift_bits in range(max(order_size.bit_length() - 1, 0)):
        parity = parity + jnp.bitwise_and(jnp.right_shift(shared_offset, shift_bits), 1)
    return (1 - 2 * jnp.bitwise_and(parity, 1)).astype(number_type)

def rotate_rows(signed):
    inner_size = min(D, 128)
    outer_size = D // inner_size
    blocks = signed.reshape(signed.shape[0], outer_size, inner_size)
    mixed_section = jnp.einsum('rab,bc->rac', blocks, hadamard_table(inner_size, jnp.float32), precision=lax.Precision.HIGHEST)
    mixed_section = jnp.einsum('rab,ca->rcb', mixed_section, hadamard_table(outer_size, jnp.float32), precision=lax.Precision.HIGHEST)
    return (mixed_section.reshape(signed.shape[0], D) * (1.0 / math.sqrt(D))).astype(jnp.bfloat16)

def reference(embeddings, sign_flips, row_order, codebook):
    subspace_width = D // SUBSPACES
    wide_input = embeddings.astype(jnp.float32)
    energy = jnp.sum(wide_input * wide_input) / ROWS
    signed = wide_input * sign_flips.astype(jnp.float32)[None, :]
    rotated = lax.map(rotate_rows, signed.reshape(ROWS // BLOCK, BLOCK, D)).reshape(ROWS, D)
    offsets = jnp.arange(ROWS, dtype=jnp.int32) // BLOCK * BLOCK
    permuted = rotated[offsets + row_order.astype(jnp.int32)]
    regrouped = permuted.reshape(ROWS // BLOCK, ROWS // ROW_DEV, PIECE, D).transpose(1, 0, 2, 3).reshape(ROWS, D)
    row_norms = lax.optimization_barrier(jnp.sum(jnp.square(regrouped.astype(jnp.float32)), axis=1))
    stretch = ANISO_GAIN * SUBSPACES * energy / (row_norms * row_norms + STABILITY_FLOOR)

    def assign(subspace):
        columns = lax.dynamic_slice_in_dim(regrouped, subspace * subspace_width, subspace_width, 1)
        centres = lax.dynamic_index_in_dim(codebook, subspace, 0, keepdims=False)
        inner_products = jnp.dot(columns, centres.T, preferred_element_type=jnp.float32)
        wide_columns = columns.astype(jnp.float32)
        own_square = lax.optimization_barrier(jnp.sum(wide_columns * wide_columns, axis=1, keepdims=True))
        wide_centres = centres.astype(jnp.float32)
        centre_square = lax.optimization_barrier(jnp.sum(wide_centres * wide_centres, axis=1))[None, :]
        parallel = own_square - inner_products
        squared_distance = own_square - 2.0 * inner_products + centre_square + stretch[:, None] * parallel * parallel
        assignment_scores = -squared_distance / SOFTNESS_LEVEL
        highest = lax.optimization_barrier(jnp.max(assignment_scores, axis=1, keepdims=True))
        raised = jnp.exp(assignment_scores - highest)
        weights = (raised / lax.optimization_barrier(jnp.sum(raised, axis=1, keepdims=True))).astype(jnp.bfloat16)
        decoded_part = jnp.dot(weights, centres, preferred_element_type=jnp.float32).astype(jnp.bfloat16)
        weighted_sums = jnp.dot(weights.T, columns, preferred_element_type=jnp.float32)
        counts = lax.optimization_barrier(jnp.sum(weights.astype(jnp.float32), axis=0))
        return (decoded_part, weighted_sums, counts)
    decoded, weighted_sums, counts = lax.map(assign, jnp.arange(SUBSPACES, dtype=jnp.int32))
    decoded = decoded.transpose(1, 0, 2).reshape(ROWS, D)
    new_codebook = (weighted_sums + PRIOR_MASS * codebook.astype(jnp.float32)) / (counts[:, :, None] + PRIOR_MASS)
    return (decoded, new_codebook)
```

```python
import math

import jax
import jax.numpy as jnp
from jax import lax
from jax.experimental import pallas as pl
from jax.experimental.pallas import tpu as pltpu
from jax.sharding import PartitionSpec as P

ANISO_GAIN = 1.0
SOFTNESS_LEVEL = 4.0
PRIOR_MASS = 1.0
STABILITY_FLOOR = 1e-06
LOG2E = math.log2(math.e)
NT = (((1,), (1,)), ((), ()))
F32 = jnp.float32
BF16 = jnp.bfloat16
LANES = 128


def hadamard(order):
    i = lax.broadcasted_iota(jnp.int32, (order, order), 0)
    j = lax.broadcasted_iota(jnp.int32, (order, order), 1)
    both = jnp.bitwise_and(i, j)
    parity = jnp.zeros((order, order), jnp.int32)
    for shift in range(order.bit_length() - 1):
        parity = parity + jnp.bitwise_and(jnp.right_shift(both, shift), 1)
    return (1 - 2 * jnp.bitwise_and(parity, 1)).astype(F32).astype(BF16)


def identity(order):
    i = lax.broadcasted_iota(jnp.int32, (order, order), 0)
    j = lax.broadcasted_iota(jnp.int32, (order, order), 1)
    return (i == j).astype(F32).astype(BF16)


def prepare_codes(m, ct_ref, c_ref, cb_ref, caug_ref):
    ct = ct_ref[m]
    width, codes = ct.shape
    wide = ct.astype(F32)
    c_ref[m] = wide.T.astype(BF16)
    square = jnp.sum(wide * wide, axis=0, keepdims=True) * (LOG2E / SOFTNESS_LEVEL)
    cb_ref[m] = jnp.broadcast_to(square, (LANES, codes)).T
    caug_ref[m, 0:width, :] = ct
    row = lax.broadcasted_iota(jnp.int32, (width, codes), 0)
    caug_ref[m, width : 2 * width, :] = jnp.where(row == 0, 1.0, 0.0).astype(BF16)


def rotate_block(block, rows, x_ref, rt_ref, own_ref, energy, width):
    outer = x_ref.shape[0]
    inner = x_ref.shape[2]
    h = hadamard(inner)
    parts = [
        lax.dot_general(h, x_ref[b, pl.ds(block * rows, rows), :], NT, preferred_element_type=F32)
        for b in range(outer)
    ]
    span = 1
    while span < outer:
        for b in range(outer):
            if not b & span:
                low, high = parts[b], parts[b | span]
                parts[b], parts[b | span] = low + high, low - high
        span *= 2
    scale = 1.0 / math.sqrt(outer * inner)
    total = jnp.zeros((1, rows), F32)
    for b in range(outer):
        rounded = (parts[b] * scale).astype(BF16)
        rt_ref[b * inner : (b + 1) * inner, :] = rounded
        wide = rounded.astype(F32)
        own = jnp.sum((wide * wide).reshape(inner // width, width, rows), axis=1)
        own_ref[b * (inner // width) : (b + 1) * (inner // width), :] = own
        total = total + jnp.sum(own, axis=0, keepdims=True)
    subspaces = outer * inner // width
    return ANISO_GAIN * subspaces * energy / (total * total + STABILITY_FLOOR)


def assign(m, rows, stretch, rt_ref, own_ref, c_ref, cb_ref, caug_ref, dt_ref, sums_ref, first):
    width = c_ref.shape[2]
    at = pl.ds(pl.multiple_of(m * width, width), width)
    x = rt_ref[at, :]
    own = own_ref[pl.ds(m, 1), :]
    g = jnp.dot(c_ref[m], x, preferred_element_type=F32)
    a = (1.0 + stretch * own) * (2.0 * LOG2E / SOFTNESS_LEVEL)
    b = stretch * (LOG2E / SOFTNESS_LEVEL)
    cb = cb_ref[m]
    t = g * (a - b * g) - jnp.concatenate([cb] * (rows // LANES), axis=1)
    e = jnp.exp2(t - jnp.max(t, axis=0, keepdims=True)).astype(BF16)
    o = jnp.dot(caug_ref[m], e, preferred_element_type=F32)
    inv = 1.0 / o[width : width + 1, :]
    dt_ref[at, :] = (o[0:width, :] * inv).astype(BF16)
    row = lax.broadcasted_iota(jnp.int32, (width, rows), 0)
    inv_high = inv.astype(BF16).astype(F32)
    tail = jnp.where(row == 0, inv_high, jnp.where(row == 1, inv - inv_high, 0.0))
    left = jnp.concatenate([x.astype(F32) * inv, tail], axis=0).astype(BF16)
    s = lax.dot_general(left, e, NT, preferred_element_type=F32)
    s = jnp.concatenate([s[0:width], s[width : width + 1] + s[width + 1 : width + 2], s[width + 1 : width + 8]], axis=0)

    sums_ref[m] = jnp.where(first, 0.0, sums_ref[m]) + s


def compute_kernel(energy_ref, x_ref, ct_ref, out_ref, sums_ref, c_ref, cb_ref, caug_ref, rt_ref, own_ref, dt_ref):
    subspaces, width, codes = ct_ref.shape
    outer, all_rows, inner = x_ref.shape
    rows = rt_ref.shape[1]
    energy = energy_ref[0, 0]

    def prep(m, carry):
        prepare_codes(m, ct_ref, c_ref, cb_ref, caug_ref)
        return carry

    lax.fori_loop(0, subspaces, prep, 0)

    def one_block(block, carry):
        stretch = rotate_block(block, rows, x_ref, rt_ref, own_ref, energy, width)

        def one(i, carry):
            for k in range(UNROLL):
                assign(
                    i * UNROLL + k, rows, stretch, rt_ref, own_ref, c_ref, cb_ref, caug_ref, dt_ref, sums_ref, block == 0
                )
            return carry

        lax.fori_loop(0, subspaces // UNROLL, one, 0)
        eye = identity(rows)
        for b in range(outer):
            flipped = lax.dot_general(eye, dt_ref[b * inner : (b + 1) * inner, :], NT, preferred_element_type=F32)
            out_ref[pl.ds(pl.multiple_of(block * rows, rows), rows), b * inner : (b + 1) * inner] = flipped.astype(BF16)
        return carry

    lax.fori_loop(0, all_rows // rows, one_block, 0)


UNROLL = 2


def compute(energy, x, ct):
    subspaces, width, codes = ct.shape
    outer, all_rows, inner = x.shape
    rows = 256
    vmem = pl.BlockSpec(memory_space=pltpu.VMEM)
    return pl.pallas_call(
        compute_kernel,
        out_shape=(
            jax.ShapeDtypeStruct((all_rows, outer * inner), BF16),
            jax.ShapeDtypeStruct((subspaces, width + 8, codes), F32),
        ),
        in_specs=[pl.BlockSpec(memory_space=pltpu.SMEM), vmem, vmem],
        out_specs=(vmem, vmem),
        scratch_shapes=[
            pltpu.VMEM((subspaces, codes, width), BF16),
            pltpu.VMEM((subspaces, codes, LANES), F32),
            pltpu.VMEM((subspaces, 2 * width, codes), BF16),
            pltpu.VMEM((outer * inner, rows), BF16),
            pltpu.VMEM((subspaces, rows), F32),
            pltpu.VMEM((outer * inner, rows), BF16),
        ],
        compiler_params=pltpu.CompilerParams(vmem_limit_bytes=48 * 1024 * 1024),
        name="assign_codes",
    )(energy, x, ct)


def body(embeddings, sign_flips, row_order, codebook):
    rows_count = lax.axis_size("rows")
    dims_count = lax.axis_size("dims")
    devices = rows_count * dims_count
    block_rows, local_width = embeddings.shape
    row_dev = block_rows // dims_count
    piece_rows = block_rows // devices
    wide_input = embeddings.astype(F32)
    energy_total = lax.psum(jnp.sum(wide_input * wide_input), ("rows", "dims"))
    energy = energy_total / (row_dev * devices)
    signed = embeddings * sign_flips.astype(BF16)[None, :]
    outgoing = signed[row_order].reshape(devices, piece_rows, local_width)
    arrived = lax.all_to_all(outgoing, ("rows", "dims"), split_axis=0, concat_axis=0, tiled=True)
    x = (
        arrived.reshape(rows_count, dims_count, piece_rows, local_width)
        .transpose(1, 0, 2, 3)
        .reshape(dims_count, row_dev, local_width)
    )
    ct = codebook.transpose(0, 2, 1)
    width = ct.shape[1]
    decoded, sums = compute(energy.reshape(1, 1), x, ct)
    sums = lax.psum(sums[:, : width + 1], ("rows", "dims"))
    new = (sums[:, :width] + PRIOR_MASS * ct.astype(F32)) / (sums[:, width : width + 1] + PRIOR_MASS)
    return decoded, new.transpose(0, 2, 1)


def solution(mesh):
    return jax.shard_map(
        body,
        mesh=mesh,
        in_specs=(P("rows", "dims"), P("dims"), P("rows"), P()),
        out_specs=(P(("rows", "dims"), None), P()),
        check_vma=False,
    )
```

```python
import math

import jax
import jax.numpy as jnp
from jax import lax
from jax.experimental import pallas as pl
from jax.experimental.pallas import tpu as pltpu
from jax.sharding import PartitionSpec as P

ANISO_GAIN = 1.0
SOFTNESS_LEVEL = 4.0
PRIOR_MASS = 1.0
STABILITY_FLOOR = 1e-06
LOG2E = math.log2(math.e)
NT = (((1,), (1,)), ((), ()))
F32 = jnp.float32
BF16 = jnp.bfloat16
LANES = 128


def hadamard(order):
    i = lax.broadcasted_iota(jnp.int32, (order, order), 0)
    j = lax.broadcasted_iota(jnp.int32, (order, order), 1)
    both = jnp.bitwise_and(i, j)
    parity = jnp.zeros((order, order), jnp.int32)
    for shift in range(order.bit_length() - 1):
        parity = parity + jnp.bitwise_and(jnp.right_shift(both, shift), 1)
    return (1 - 2 * jnp.bitwise_and(parity, 1)).astype(F32).astype(BF16)


def identity(order):
    i = lax.broadcasted_iota(jnp.int32, (order, order), 0)
    j = lax.broadcasted_iota(jnp.int32, (order, order), 1)
    return (i == j).astype(F32).astype(BF16)


def prepare_codes(m, ct_ref, c_ref, cb_ref, caug_ref):
    ct = ct_ref[m]
    width, codes = ct.shape
    wide = ct.astype(F32)
    c_ref[m] = wide.T.astype(BF16)
    square = jnp.sum(wide * wide, axis=0, keepdims=True) * (LOG2E / SOFTNESS_LEVEL)
    cb_ref[m] = jnp.broadcast_to(square, (LANES, codes)).T
    caug_ref[m, 0:width, :] = ct
    row = lax.broadcasted_iota(jnp.int32, (width, codes), 0)
    caug_ref[m, width : 2 * width, :] = jnp.where(row == 0, 1.0, 0.0).astype(BF16)


def rotate_block(block, rows, x_ref, rt_ref, own_ref, energy, width):
    outer = x_ref.shape[0]
    inner = x_ref.shape[2]
    h = hadamard(inner)
    parts = [
        lax.dot_general(h, x_ref[b, pl.ds(block * rows, rows), :], NT, preferred_element_type=F32)
        for b in range(outer)
    ]
    span = 1
    while span < outer:
        for b in range(outer):
            if not b & span:
                low, high = parts[b], parts[b | span]
                parts[b], parts[b | span] = low + high, low - high
        span *= 2
    scale = 1.0 / math.sqrt(outer * inner)
    total = jnp.zeros((1, rows), F32)
    for b in range(outer):
        rounded = (parts[b] * scale).astype(BF16)
        rt_ref[b * inner : (b + 1) * inner, :] = rounded
        wide = rounded.astype(F32)
        own = jnp.sum((wide * wide).reshape(inner // width, width, rows), axis=1)
        own_ref[b * (inner // width) : (b + 1) * (inner // width), :] = own
        total = total + jnp.sum(own, axis=0, keepdims=True)
    subspaces = outer * inner // width
    return ANISO_GAIN * subspaces * energy / (total * total + STABILITY_FLOOR)


def assign(ms, rows, stretch, rt_ref, own_ref, c_ref, cb_ref, caug_ref, dt_ref, sums_ref, first):
    width = c_ref.shape[2]
    ats = [pl.ds(pl.multiple_of(m * width, width), width) for m in ms]
    xs = [rt_ref[at, :] for at in ats]
    gs = [jnp.dot(c_ref[m], x, preferred_element_type=F32) for m, x in zip(ms, xs)]
    b = stretch * (LOG2E / SOFTNESS_LEVEL)
    es = []
    for m, g in zip(ms, gs):
        a = (1.0 + stretch * own_ref[pl.ds(m, 1), :]) * (2.0 * LOG2E / SOFTNESS_LEVEL)
        t = g * (a - b * g) - jnp.concatenate([cb_ref[m]] * (rows // LANES), axis=1)
        es.append(jnp.exp2(t - jnp.max(t, axis=0, keepdims=True)).astype(BF16))
    os = [jnp.dot(caug_ref[m], e, preferred_element_type=F32) for m, e in zip(ms, es)]
    row = lax.broadcasted_iota(jnp.int32, (width, rows), 0)
    lefts = []
    for at, o, x in zip(ats, os, xs):
        inv = 1.0 / o[width : width + 1, :]
        dt_ref[at, :] = (o[0:width, :] * inv).astype(BF16)
        inv_high = inv.astype(BF16).astype(F32)
        tail = jnp.where(row == 0, inv_high, jnp.where(row == 1, inv - inv_high, 0.0))
        lefts.append(jnp.concatenate([x.astype(F32) * inv, tail], axis=0).astype(BF16))
    ss = [lax.dot_general(left, e, NT, preferred_element_type=F32) for left, e in zip(lefts, es)]
    for m, s in zip(ms, ss):
        s = jnp.concatenate(
            [s[0:width], s[width : width + 1] + s[width + 1 : width + 2], s[width + 1 : width + 8]], axis=0
        )
        sums_ref[m] = jnp.where(first, 0.0, sums_ref[m]) + s


def compute_kernel(energy_ref, x_ref, ct_ref, out_ref, sums_ref, c_ref, cb_ref, caug_ref, rt_ref, own_ref, dt_ref):
    subspaces, width, codes = ct_ref.shape
    outer, all_rows, inner = x_ref.shape
    rows = rt_ref.shape[1]
    energy = energy_ref[0, 0]

    def prep(m, carry):
        prepare_codes(m, ct_ref, c_ref, cb_ref, caug_ref)
        return carry

    lax.fori_loop(0, subspaces, prep, 0)

    def one_block(block, carry):
        stretch = rotate_block(block, rows, x_ref, rt_ref, own_ref, energy, width)

        def one(i, carry):
            ms = [i * UNROLL + k for k in range(UNROLL)]
            assign(ms, rows, stretch, rt_ref, own_ref, c_ref, cb_ref, caug_ref, dt_ref, sums_ref, block == 0)
            return carry

        lax.fori_loop(0, subspaces // UNROLL, one, 0)
        eye = identity(rows)
        for b in range(outer):
            flipped = lax.dot_general(eye, dt_ref[b * inner : (b + 1) * inner, :], NT, preferred_element_type=F32)
            out_ref[pl.ds(pl.multiple_of(block * rows, rows), rows), b * inner : (b + 1) * inner] = flipped.astype(BF16)
        return carry

    lax.fori_loop(0, all_rows // rows, one_block, 0)


UNROLL = 8


def compute(energy, x, ct):
    subspaces, width, codes = ct.shape
    outer, all_rows, inner = x.shape
    rows = 256
    vmem = pl.BlockSpec(memory_space=pltpu.VMEM)
    return pl.pallas_call(
        compute_kernel,
        out_shape=(
            jax.ShapeDtypeStruct((all_rows, outer * inner), BF16),
            jax.ShapeDtypeStruct((subspaces, width + 8, codes), F32),
        ),
        in_specs=[pl.BlockSpec(memory_space=pltpu.SMEM), vmem, vmem],
        out_specs=(vmem, vmem),
        scratch_shapes=[
            pltpu.VMEM((subspaces, codes, width), BF16),
            pltpu.VMEM((subspaces, codes, LANES), F32),
            pltpu.VMEM((subspaces, 2 * width, codes), BF16),
            pltpu.VMEM((outer * inner, rows), BF16),
            pltpu.VMEM((subspaces, rows), F32),
            pltpu.VMEM((outer * inner, rows), BF16),
        ],
        compiler_params=pltpu.CompilerParams(vmem_limit_bytes=48 * 1024 * 1024),
        name="assign_codes",
    )(energy, x, ct)


MESH = pl.DeviceIdType.MESH


def wait_bytes(ref, sem):
    pltpu.make_async_copy(ref, ref, sem).wait()


def regroup_kernel(
    emb_ref, sign_ref, order_ref, x_ref, energy_ref,
    wide, stage, send, part, part_rows, got_dims, got_rows,
    send_sem, recv_sem, esend_dims, erecv_dims, esend_rows, erecv_rows,
):
    r, d = lax.axis_index("rows"), lax.axis_index("dims")
    n_rows, n_dims = lax.axis_size("rows"), lax.axis_size("dims")
    devices, piece, inner = send.shape
    block = emb_ref.shape[0]

    barrier = pltpu.get_barrier_semaphore()

    def greet(i, carry):
        step = i + 1
        there = lax.rem(r * n_dims + d + step, devices)
        pl.semaphore_signal(barrier, inc=1, device_id=(there // n_dims, lax.rem(there, n_dims)), device_id_type=MESH)
        return carry

    lax.fori_loop(0, devices - 1, greet, 0)

    sign = sign_ref[...].astype(F32)
    chunk = 256

    def widen(i, acc):
        at = pl.ds(pl.multiple_of(i * chunk, chunk), chunk)
        v = emb_ref[at, :].astype(F32)
        wide[at, :] = v * sign
        return acc + jnp.sum((v * v).reshape(chunk // 8, 8, inner), axis=0)

    part[...] = lax.fori_loop(0, block // chunk, widen, jnp.zeros((8, inner), F32))
    pl.semaphore_wait(barrier, devices - 1)

    def energy_copy(axis, src, dst, there, send_s, recv_s):
        return pltpu.make_async_remote_copy(
            src_ref=src, dst_ref=dst, send_sem=send_s, recv_sem=recv_s, device_id=there, device_id_type=MESH
        )

    for k in range(1, n_dims):
        there = lax.rem(d + k, n_dims)
        energy_copy(1, part, got_dims.at[k], (r, there), esend_dims.at[k], erecv_dims.at[k]).start()

    def gather(j, k, slot):
        to_r, to_d = lax.rem(r + j, n_rows), lax.rem(d + k, n_dims)
        q = to_r * n_dims + to_d
        first = q * piece
        for u in range(piece):
            stage[slot, pl.ds(u, 1), :] = wide[pl.ds(order_ref[first + u], 1), :]
        send[q] = stage[slot].astype(BF16)
        here = x_ref.at[d, pl.ds(pl.multiple_of(r * piece, piece), piece), :]
        return q, here, to_r, to_d

    def one_piece(j, k, slot):
        q, here, to_r, to_d = gather(j, k, slot)
        pltpu.make_async_remote_copy(
            src_ref=send.at[q], dst_ref=here, send_sem=send_sem.at[j], recv_sem=recv_sem.at[j],
            device_id=(to_r, to_d), device_id_type=MESH,
        ).start()

    def group(j, carry):
        def pair(i, carry):
            for slot in range(2):
                one_piece(j, i * 2 + slot, slot)
            return carry

        lax.fori_loop(0, n_dims // 2, pair, 0)
        return carry

    q, here = gather(0, 0, 0)[:2]
    pltpu.make_async_copy(send.at[q], here, recv_sem.at[0]).start()
    for k in range(1, n_dims):
        one_piece(0, k, k % 2)
    lax.fori_loop(1, n_rows // 4, group, 0)

    total = part[...]
    for k in range(1, n_dims):
        wait_bytes(part, erecv_dims.at[k])
        total = total + got_dims[k]
    part_rows[...] = total
    for k in range(1, n_rows):
        there = lax.rem(r + k, n_rows)
        energy_copy(0, part_rows, got_rows.at[k], (there, d), esend_rows.at[k], erecv_rows.at[k]).start()
    lax.fori_loop(n_rows // 4, n_rows, group, 0)
    for k in range(1, n_rows):
        wait_bytes(part, erecv_rows.at[k])
        total = total + got_rows[k]
    energy_ref[...] = jnp.broadcast_to(jnp.sum(total, keepdims=True), energy_ref.shape) / (block * n_rows)

    wait_bytes(send.at[pl.ds(0, n_dims - 1)], send_sem.at[0])
    for j in range(n_rows):
        if j:
            wait_bytes(send.at[pl.ds(0, n_dims)], send_sem.at[j])
        at = pl.ds(pl.multiple_of(lax.rem(r + n_rows - j, n_rows) * piece, piece), piece)
        wait_bytes(x_ref.at[:, at, :], recv_sem.at[j])
    for k in range(1, n_dims):
        wait_bytes(part, esend_dims.at[k])
    for k in range(1, n_rows):
        wait_bytes(part, esend_rows.at[k])


def regroup(embeddings, sign_flips, row_order):
    n_rows, n_dims = lax.axis_size("rows"), lax.axis_size("dims")
    block, inner = embeddings.shape
    devices = n_rows * n_dims
    piece = block // devices
    vmem = pl.BlockSpec(memory_space=pltpu.VMEM)
    dma = pltpu.SemaphoreType.DMA
    return pl.pallas_call(
        regroup_kernel,
        out_shape=(
            jax.ShapeDtypeStruct((n_dims, block // n_dims, inner), BF16),
            jax.ShapeDtypeStruct((8, inner), F32),
        ),
        in_specs=[vmem, vmem, pl.BlockSpec(memory_space=pltpu.SMEM)],
        out_specs=(vmem, vmem),
        scratch_shapes=[
            pltpu.VMEM((block, inner), F32),
            pltpu.VMEM((2, piece, inner), F32),
            pltpu.VMEM((devices, piece, inner), BF16),
            pltpu.VMEM((8, inner), F32),
            pltpu.VMEM((8, inner), F32),
            pltpu.VMEM((n_dims, 8, inner), F32),
            pltpu.VMEM((n_rows, 8, inner), F32),
            dma((n_rows,)),
            dma((n_rows,)),
            dma((n_dims,)),
            dma((n_dims,)),
            dma((n_rows,)),
            dma((n_rows,)),
        ],
        compiler_params=pltpu.CompilerParams(
            collective_id=0, has_side_effects=True, vmem_limit_bytes=32 * 1024 * 1024
        ),
        name="regroup_rows",
    )(embeddings, sign_flips.reshape(1, inner), row_order)


def combine_kernel(
    sums_ref, ct_ref, out_ref, low, counts, got_low, got_counts, both, got_both,
    sem_a, sem_b, sem_c, sem_d, sem_e, sem_f, sem_g, sem_h, sem_i, sem_j,
):
    r, d = lax.axis_index("rows"), lax.axis_index("dims")
    n_rows, n_dims = lax.axis_size("rows"), lax.axis_size("dims")
    subspaces, width, codes = ct_ref.shape
    group = subspaces // n_dims
    half = codes * group // n_rows

    barrier = pltpu.get_barrier_semaphore()
    for k in range(1, n_dims):
        pl.semaphore_signal(barrier, inc=1, device_id=(r, lax.rem(d + k, n_dims)), device_id_type=MESH)
    for k in range(1, n_rows):
        pl.semaphore_signal(barrier, inc=1, device_id=(lax.rem(r + k, n_rows), d), device_id_type=MESH)

    for s in range(subspaces):
        low[s] = sums_ref[s, 0:width, :].astype(BF16)
        counts[s : s + 1, :] = sums_ref[s, width : width + 1, :]
    pl.semaphore_wait(barrier, n_dims + n_rows - 2)

    def remote(src, dst, there, send_s, recv_s):
        return pltpu.make_async_remote_copy(
            src_ref=src, dst_ref=dst, send_sem=send_s, recv_sem=recv_s, device_id=there, device_id_type=MESH
        )

    sent = []

    def go(*args):
        copy = remote(*args)
        copy.start()
        sent.append(copy)

    for k in range(1, n_dims):
        there = lax.rem(d + k, n_dims)
        at = pl.ds(pl.multiple_of(there * group, group), group)
        go(low.at[at], got_low.at[k], (r, there), sem_a.at[k], sem_b.at[k])
        go(counts.at[at], got_counts.at[k], (r, there), sem_c.at[k], sem_d.at[k])
    mine = pl.ds(pl.multiple_of(d * group, group), group)
    total = sums_ref[mine, 0:width, :]
    total_counts = counts[mine, :]
    for k in range(1, n_dims):
        wait_bytes(got_low.at[k], sem_b.at[k])
        wait_bytes(got_counts.at[k], sem_d.at[k])
        total = total + got_low[k].astype(F32)
        total_counts = total_counts + got_counts[k]
    for s in range(group):
        for h in range(codes // half):
            lanes = slice(h * half, (h + 1) * half)
            both[s * (codes // half) + h, 0:width, :] = total[s, :, lanes]
            both[s * (codes // half) + h, width : width + 8, :] = jnp.broadcast_to(total_counts[s : s + 1, lanes], (8, half))
    for k in range(1, n_rows):
        there = lax.rem(r + k, n_rows)
        go(both.at[there], got_both.at[k], (there, d), sem_e.at[k], sem_f.at[k])
    total = both[r]
    for k in range(1, n_rows):
        wait_bytes(got_both.at[k], sem_f.at[k])
        total = total + got_both[k]

    def place(rank):
        return d * group + rank // (codes // half), pl.ds(pl.multiple_of(lax.rem(rank, codes // half) * half, half), half)

    s, lanes = place(r)
    out_ref[s, :, lanes] = (total[0:width] + PRIOR_MASS * ct_ref[s, :, lanes].astype(F32)) / (
        total[width : width + 1] + PRIOR_MASS
    )
    for k in range(1, n_rows):
        there = lax.rem(r + k, n_rows)
        go(out_ref.at[s, :, lanes], out_ref.at[s, :, lanes], (there, d), sem_g.at[k], sem_h.at[k])
    for k in range(1, n_rows):
        s, lanes = place(lax.rem(r + n_rows - k, n_rows))
        wait_bytes(out_ref.at[s, :, lanes], sem_h.at[k])
    for k in range(1, n_dims):
        go(out_ref.at[mine], out_ref.at[mine], (r, lax.rem(d + k, n_dims)), sem_i.at[k], sem_j.at[k])
    for k in range(1, n_dims):
        there = lax.rem(d + n_dims - k, n_dims)
        wait_bytes(out_ref.at[pl.ds(pl.multiple_of(there * group, group), group)], sem_j.at[k])
    for copy in sent:
        copy.wait_send()


def combine(sums, ct):
    n_rows, n_dims = lax.axis_size("rows"), lax.axis_size("dims")
    subspaces, width, codes = ct.shape
    group = subspaces // n_dims
    half = codes * group // n_rows
    vmem = pl.BlockSpec(memory_space=pltpu.VMEM)
    dma = pltpu.SemaphoreType.DMA
    return pl.pallas_call(
        combine_kernel,
        out_shape=jax.ShapeDtypeStruct((subspaces, width, codes), F32),
        in_specs=[vmem, vmem],
        out_specs=vmem,
        scratch_shapes=[
            pltpu.VMEM((subspaces, width, codes), BF16),
            pltpu.VMEM((subspaces, codes), F32),
            pltpu.VMEM((n_dims, group, width, codes), BF16),
            pltpu.VMEM((n_dims, group, codes), F32),
            pltpu.VMEM((n_rows, width + 8, half), F32),
            pltpu.VMEM((n_rows, width + 8, half), F32),
        ]
        + [dma((n_dims,))] * 4
        + [dma((n_rows,))] * 4
        + [dma((n_dims,))] * 2,
        compiler_params=pltpu.CompilerParams(
            collective_id=1, has_side_effects=True, vmem_limit_bytes=32 * 1024 * 1024
        ),
        name="combine_sums",
    )(sums, ct)


def body(embeddings, sign_flips, row_order, codebook):
    ct = codebook.transpose(0, 2, 1)
    x, energy = regroup(embeddings, sign_flips, row_order)
    decoded, sums = compute(energy, x, ct)
    return decoded, combine(sums, ct).transpose(0, 2, 1)


def solution(mesh):
    return jax.shard_map(
        body,
        mesh=mesh,
        in_specs=(P("rows", "dims"), P("dims"), P("rows"), P()),
        out_specs=(P(("rows", "dims"), None), P()),
        check_vma=False,
    )
```

```python
import math

import jax
import jax.numpy as jnp
from jax import lax
from jax.experimental import pallas as pl
from jax.experimental.pallas import tpu as pltpu
from jax.sharding import PartitionSpec as P

ANISO_GAIN = 1.0
SOFTNESS_LEVEL = 4.0
PRIOR_MASS = 1.0
STABILITY_FLOOR = 1e-06
LOG2E = math.log2(math.e)
NT = (((1,), (1,)), ((), ()))
F32 = jnp.float32
BF16 = jnp.bfloat16
LANES = 128


def hadamard(order):
    i = lax.broadcasted_iota(jnp.int32, (order, order), 0)
    j = lax.broadcasted_iota(jnp.int32, (order, order), 1)
    both = jnp.bitwise_and(i, j)
    parity = jnp.zeros((order, order), jnp.int32)
    for shift in range(order.bit_length() - 1):
        parity = parity + jnp.bitwise_and(jnp.right_shift(both, shift), 1)
    return (1 - 2 * jnp.bitwise_and(parity, 1)).astype(F32).astype(BF16)


def identity(order):
    i = lax.broadcasted_iota(jnp.int32, (order, order), 0)
    j = lax.broadcasted_iota(jnp.int32, (order, order), 1)
    return (i == j).astype(F32).astype(BF16)


def prepare_codes(m, ct_ref, c_ref, cb_ref, caug_ref):
    ct = ct_ref[m]
    width, codes = ct.shape
    wide = ct.astype(F32)
    c_ref[m] = wide.T.astype(BF16)
    square = jnp.sum(wide * wide, axis=0, keepdims=True) * (LOG2E / SOFTNESS_LEVEL)
    cb_ref[m] = jnp.broadcast_to(square, (LANES, codes)).T
    caug_ref[m, 0:width, :] = ct
    row = lax.broadcasted_iota(jnp.int32, (width, codes), 0)
    caug_ref[m, width : 2 * width, :] = jnp.where(row == 0, 1.0, 0.0).astype(BF16)


def rotate_block(block, rows, x_ref, rt_ref, own_ref, energy, width):
    outer = x_ref.shape[0]
    inner = x_ref.shape[2]
    h = hadamard(inner)
    parts = [
        lax.dot_general(h, x_ref[b, pl.ds(pl.multiple_of(block * rows, rows), rows), :], NT, preferred_element_type=F32)
        for b in range(outer)
    ]
    span = 1
    while span < outer:
        for b in range(outer):
            if not b & span:
                low, high = parts[b], parts[b | span]
                parts[b], parts[b | span] = low + high, low - high
        span *= 2
    scale = 1.0 / math.sqrt(outer * inner)
    total = jnp.zeros((1, rows), F32)
    for b in range(outer):
        rounded = (parts[b] * scale).astype(BF16)
        rt_ref[b * inner : (b + 1) * inner, :] = rounded
        wide = rounded.astype(F32)
        own = jnp.sum((wide * wide).reshape(inner // width, width, rows), axis=1)
        own_ref[b * (inner // width) : (b + 1) * (inner // width), :] = own
        total = total + jnp.sum(own, axis=0, keepdims=True)
    subspaces = outer * inner // width
    return ANISO_GAIN * subspaces * energy / (total * total + STABILITY_FLOOR)


def assign(ms, rows, stretch, rt_ref, own_ref, c_ref, cb_ref, caug_ref, dt_ref, sums_ref):
    width = c_ref.shape[2]
    ats = [pl.ds(pl.multiple_of(m * width, width), width) for m in ms]
    xs = [rt_ref[at, :] for at in ats]
    gs = [jnp.dot(c_ref[m], x, preferred_element_type=F32) for m, x in zip(ms, xs)]
    b = stretch * (LOG2E / SOFTNESS_LEVEL)
    es = []
    for m, g in zip(ms, gs):
        a = (1.0 + stretch * own_ref[pl.ds(m, 1), :]) * (2.0 * LOG2E / SOFTNESS_LEVEL)
        t = g * (a - b * g) - jnp.concatenate([cb_ref[m]] * (rows // LANES), axis=1)
        es.append(jnp.exp2(t - jnp.max(t, axis=0, keepdims=True)).astype(BF16))
    os = [jnp.dot(caug_ref[m], e, preferred_element_type=F32) for m, e in zip(ms, es)]
    row = lax.broadcasted_iota(jnp.int32, (width, rows), 0)
    lefts = []
    for at, o, x in zip(ats, os, xs):
        inv = 1.0 / o[width : width + 1, :]
        dt_ref[at, :] = (o[0:width, :] * inv).astype(BF16)
        inv_high = inv.astype(BF16).astype(F32)
        tail = jnp.where(row == 0, inv_high, jnp.where(row == 1, inv - inv_high, 0.0))
        lefts.append(jnp.concatenate([x.astype(F32) * inv, tail], axis=0).astype(BF16))
    ss = [lax.dot_general(left, e, NT, preferred_element_type=F32) for left, e in zip(lefts, es)]
    for m, s in zip(ms, ss):
        s = jnp.concatenate(
            [s[0:width], s[width : width + 1] + s[width + 1 : width + 2], s[width + 1 : width + 8]], axis=0
        )
        sums_ref[m] = sums_ref[m] + s


MESH = pl.DeviceIdType.MESH
GROUP = 8
SIDE = 4


def wait_bytes(ref, sem):
    pltpu.make_async_copy(ref, ref, sem).wait()


def remote(src, dst, there, send_sem, recv_sem):
    return pltpu.make_async_remote_copy(
        src_ref=src, dst_ref=dst, send_sem=send_sem, recv_sem=recv_sem, device_id=there, device_id_type=MESH
    )


def kernel(
    emb_hbm, sign_ref, order_hbm, ct_hbm, out_hbm, new_ref,
    emb_ref, order_ref, ct_ref, wide, send, x_ref,
    part, part_rows, got_dims, got_rows,
    c_ref, cb_ref, caug_ref, rt_ref, own_ref, dt_ref, dec_ref, sums_ref,
    low, counts, got_low, got_counts, both, got_both, piece_ref, all_ref,
    load_sem, emb_sem, send_sem, recv_sem, store_sem, esend_dims, erecv_dims, esend_rows, erecv_rows,
    sem_a, sem_b, sem_c, sem_d, sem_e, sem_f, sem_g, sem_h, sem_i, sem_j,
):
    r, d = lax.axis_index("rows"), lax.axis_index("dims")
    n_rows, n_dims = lax.axis_size("rows"), lax.axis_size("dims")
    devices, piece, inner = send.shape
    block = emb_ref.shape[0]
    subspaces, width, codes = ct_ref.shape
    outer, all_rows, _ = x_ref.shape
    rows = rt_ref.shape[1]
    blocks = all_rows // rows
    per_block = rows // piece
    chunks = emb_sem.shape[0]
    chunk = block // chunks

    order_load = pltpu.make_async_copy(order_hbm, order_ref, load_sem.at[0])
    ct_load = pltpu.make_async_copy(ct_hbm, ct_ref, load_sem.at[1])

    def emb_load(i):
        at = pl.ds(pl.multiple_of(i * chunk, chunk), chunk)
        return pltpu.make_async_copy(emb_hbm.at[at], emb_ref.at[at], emb_sem.at[i])

    for i in range(chunks):
        emb_load(i).start()
    order_load.start()
    ct_load.start()

    barrier = pltpu.get_barrier_semaphore()

    def greet(i, carry):
        there = lax.rem(r * n_dims + d + i, devices)
        pl.semaphore_signal(barrier, inc=1, device_id=(there // n_dims, lax.rem(there, n_dims)), device_id_type=MESH)
        return carry

    lax.fori_loop(1, devices, greet, 0)

    sign = sign_ref[...].astype(F32)

    def widen(i, acc):
        emb_load(i).wait()
        step = 256
        for h in range(chunk // step):
            at = pl.ds(pl.multiple_of(i * chunk + h * step, step), step)
            v = emb_ref[at, :].astype(F32)
            wide[at, :] = v * sign
            acc = acc + jnp.sum((v * v).reshape(step // 8, 8, inner), axis=0)
        return acc

    part[...] = lax.fori_loop(0, chunks, widen, jnp.zeros((8, inner), F32))
    order_load.wait()
    pl.semaphore_wait(barrier, devices - 1)

    for k in range(1, n_dims):
        there = (r, lax.rem(d + k, n_dims))
        remote(part, got_dims.at[k], there, esend_dims.at[k], erecv_dims.at[k]).start()

    def target(s, i, k):
        to_z = lax.rem(r // SIDE + i, SIDE)
        to_x = lax.rem(r + s + SIDE - i, SIDE)
        return to_z * SIDE + to_x, lax.rem(d + k + 2 * i, n_dims)

    def slot(s, i):
        return pl.ds(pl.multiple_of((s * per_block + i) * piece, piece), piece)

    def gather(s, i, k):
        to_r, to_d = target(s, i, k)
        q = to_r * n_dims + to_d
        first = q * piece
        for v in range(0, piece, 16):
            got = [wide[pl.ds(order_ref[first + v + u], 1), :] for u in range(16)]
            send[q, v : v + 16, :] = jnp.concatenate(got, axis=0).astype(BF16)
        return q, to_r, to_d

    def one_piece(s, i, k):
        q, to_r, to_d = gather(s, i, k)
        remote(send.at[q], x_ref.at[d, slot(s, i), :], (to_r, to_d), send_sem.at[s], recv_sem.at[s]).start()

    q, _, _ = gather(0, 0, 0)
    pltpu.make_async_copy(send.at[q], x_ref.at[d, slot(0, 0), :], recv_sem.at[0]).start()
    for i in range(1, per_block):
        one_piece(0, i, 0)

    def across(s, low_k):
        def step(k, carry):
            for i in range(per_block):
                one_piece(s, i, k)
            return carry

        lax.fori_loop(low_k, n_dims, step, 0)

    across(0, 1)
    total = part[...]
    for k in range(1, n_dims):
        wait_bytes(part, erecv_dims.at[k])
        total = total + got_dims[k]
    part_rows[...] = total
    for k in range(1, n_rows):
        there = (lax.rem(r + k, n_rows), d)
        remote(part_rows, got_rows.at[k], there, esend_rows.at[k], erecv_rows.at[k]).start()

    def later(s, carry):
        across(s, 0)
        return carry

    lax.fori_loop(1, blocks, later, 0)

    ct_load.wait()

    def prep(m, carry):
        prepare_codes(m, ct_ref, c_ref, cb_ref, caug_ref)
        sums_ref[m] = jnp.zeros(sums_ref.shape[1:], F32)
        return carry

    lax.fori_loop(0, subspaces, prep, 0)

    for k in range(1, n_rows):
        wait_bytes(part, erecv_rows.at[k])
        total = total + got_rows[k]
    energy = jnp.sum(total, keepdims=True) / (block * n_rows)

    def store(s, i):
        from_z = lax.rem(r // SIDE + SIDE - i, SIDE)
        from_x = lax.rem(r + 2 * SIDE - s + i, SIDE)
        at = pl.ds(pl.multiple_of((from_z * SIDE + from_x) * piece, piece), piece)
        return pltpu.make_async_copy(dec_ref.at[s, pl.ds(i * piece, piece), :], out_hbm.at[at, :], store_sem.at[s, i])

    def group_sums(k):
        there = lax.rem(d + k, n_dims)
        at = pl.ds(pl.multiple_of(there * GROUP, GROUP), GROUP)
        to = (r, there)
        return (
            remote(low.at[at], got_low.at[k], to, sem_a.at[k], sem_b.at[k]),
            remote(counts.at[at], got_counts.at[k], to, sem_c.at[k], sem_d.at[k]),
        )

    def one_block(s, carry):
        wait_bytes(x_ref.at[:, pl.ds(pl.multiple_of(s * rows, rows), rows), :], recv_sem.at[s])
        stretch = rotate_block(s, rows, x_ref, rt_ref, own_ref, energy, width)

        def one_group(k, carry):
            there = lax.rem(d + k, n_dims)
            ms = [there * GROUP + i for i in range(GROUP)]
            assign(ms, rows, stretch, rt_ref, own_ref, c_ref, cb_ref, caug_ref, dt_ref, sums_ref)

            @pl.when(jnp.logical_and(s == blocks - 1, k < n_dims))
            def _():
                for m in ms:
                    low[m] = sums_ref[m, 0:width, :].astype(BF16)
                    counts[pl.ds(m, 1), :] = sums_ref[m, width : width + 1, :]
                for copy in group_sums(k):
                    copy.start()

            return carry

        lax.fori_loop(1, n_dims + 1, one_group, 0)
        eye = identity(rows)
        for b in range(outer):
            lanes = slice(b * inner, (b + 1) * inner)
            flipped = lax.dot_general(eye, dt_ref[lanes, :], NT, preferred_element_type=F32)
            dec_ref[s, :, lanes] = flipped.astype(BF16)
        for i in range(per_block):
            store(s, i).start()
        return carry

    lax.fori_loop(0, blocks, one_block, 0)

    group = subspaces // n_dims
    half = codes * group // n_rows
    halves = codes // half
    sent = []

    def go(*args):
        copy = remote(*args)
        copy.start()
        sent.append(copy)

    mine = pl.ds(pl.multiple_of(d * group, group), group)
    total = sums_ref[mine, 0:width, :]
    total_counts = sums_ref[mine, width, :]
    for k in range(1, n_dims):
        wait_bytes(got_low.at[k], sem_b.at[k])
        wait_bytes(got_counts.at[k], sem_d.at[k])
        total = total + got_low[k].astype(F32)
        total_counts = total_counts + got_counts[k]
    for g in range(group):
        for h in range(halves):
            lanes = slice(h * half, (h + 1) * half)
            both[g * halves + h, 0:width, :] = total[g, :, lanes]
            both[g * halves + h, width : width + 8, :] = jnp.broadcast_to(total_counts[g : g + 1, lanes], (8, half))
    for k in range(1, n_rows):
        there = lax.rem(r + k, n_rows)
        go(both.at[there], got_both.at[k], (there, d), sem_e.at[k], sem_f.at[k])
    total = both[r]
    for k in range(1, n_rows):
        wait_bytes(got_both.at[k], sem_f.at[k])
        total = total + got_both[k]

    own_g = d * group + r // halves
    own_lanes = pl.ds(pl.multiple_of(lax.rem(r, halves) * half, half), half)
    new = (total[0:width] + PRIOR_MASS * ct_ref[own_g, :, own_lanes].astype(F32)) / (
        total[width : width + 1] + PRIOR_MASS
    )
    all_ref[d, r] = new
    for k in range(1, n_rows):
        there = lax.rem(r + k, n_rows)
        go(all_ref.at[d, r], all_ref.at[d, r], (there, d), sem_g.at[k], sem_h.at[k])
    for k in range(1, n_rows):
        wait_bytes(all_ref.at[d, lax.rem(r + n_rows - k, n_rows)], sem_h.at[k])
    for k in range(1, n_dims):
        go(all_ref.at[d], all_ref.at[d], (r, lax.rem(d + k, n_dims)), sem_i.at[k], sem_j.at[k])
    for k in range(1, n_dims):
        wait_bytes(all_ref.at[lax.rem(d + n_dims - k, n_dims)], sem_j.at[k])
    for e in range(n_dims):
        for g in range(group):
            for h in range(halves):
                new_ref[e * group + g, :, h * half : (h + 1) * half] = all_ref[e, g * halves + h].astype(F32)

    for copy in sent:
        copy.wait_send()
    for k in range(1, n_dims):
        for copy in group_sums(k):
            copy.wait_send()
        wait_bytes(part, esend_dims.at[k])
    for k in range(1, n_rows):
        wait_bytes(part, esend_rows.at[k])
    for s in range(blocks):
        wait_bytes(send.at[pl.ds(0, per_block * n_dims - (s == 0))], send_sem.at[s])
        for i in range(per_block):
            store(s, i).wait()


def body(embeddings, sign_flips, row_order, codebook):
    ct = codebook.transpose(0, 2, 1)
    n_rows, n_dims = lax.axis_size("rows"), lax.axis_size("dims")
    block, inner = embeddings.shape
    devices = n_rows * n_dims
    piece = block // devices
    subspaces, width, codes = ct.shape
    all_rows = block // n_dims
    rows = 256
    blocks = all_rows // rows
    group = subspaces // n_dims
    half = codes * group // n_rows
    full = n_dims * inner
    vmem = pl.BlockSpec(memory_space=pltpu.VMEM)
    hbm = pl.BlockSpec(memory_space=pl.ANY)
    dma = pltpu.SemaphoreType.DMA
    decoded, new = pl.pallas_call(
        kernel,
        out_shape=(
            jax.ShapeDtypeStruct((all_rows, full), BF16),
            jax.ShapeDtypeStruct((subspaces, width, codes), F32),
        ),
        in_specs=[hbm, vmem, hbm, hbm],
        out_specs=(hbm, vmem),
        scratch_shapes=[
            pltpu.VMEM((block, inner), BF16),
            pltpu.SMEM((block,), jnp.int32),
            pltpu.VMEM((subspaces, width, codes), BF16),
            pltpu.VMEM((block, inner), F32),
            pltpu.VMEM((devices, piece, inner), BF16),
            pltpu.VMEM((n_dims, all_rows, inner), BF16),
            pltpu.VMEM((8, inner), F32),
            pltpu.VMEM((8, inner), F32),
            pltpu.VMEM((n_dims, 8, inner), F32),
            pltpu.VMEM((n_rows, 8, inner), F32),
            pltpu.VMEM((subspaces, codes, width), BF16),
            pltpu.VMEM((subspaces, codes, LANES), F32),
            pltpu.VMEM((subspaces, 2 * width, codes), BF16),
            pltpu.VMEM((full, rows), BF16),
            pltpu.VMEM((subspaces, rows), F32),
            pltpu.VMEM((full, rows), BF16),
            pltpu.VMEM((blocks, rows, full), BF16),
            pltpu.VMEM((subspaces, width + 8, codes), F32),
            pltpu.VMEM((subspaces, width, codes), BF16),
            pltpu.VMEM((subspaces, codes), F32),
            pltpu.VMEM((n_dims, group, width, codes), BF16),
            pltpu.VMEM((n_dims, group, codes), F32),
            pltpu.VMEM((n_rows, width + 8, half), F32),
            pltpu.VMEM((n_rows, width + 8, half), F32),
            pltpu.VMEM((width, half), F32),
            pltpu.VMEM((n_dims, n_rows, width, half), F32),
            dma((2,)),
            dma((8,)),
            dma((blocks,)),
            dma((blocks,)),
            dma((blocks, rows // piece)),
        ]
        + [dma((n_dims,))] * 2
        + [dma((n_rows,))] * 2
        + [dma((n_dims,))] * 4
        + [dma((n_rows,))] * 4
        + [dma((n_dims,))] * 2,
        compiler_params=pltpu.CompilerParams(
            collective_id=0, has_side_effects=True, vmem_limit_bytes=56 * 1024 * 1024
        ),
        name="update_codes",
    )(embeddings, sign_flips.reshape(1, inner), row_order, ct)
    return decoded, new.transpose(0, 2, 1)


def solution(mesh):
    return jax.shard_map(
        body,
        mesh=mesh,
        in_specs=(P("rows", "dims"), P("dims"), P("rows"), P()),
        out_specs=(P(("rows", "dims"), None), P()),
        check_vma=False,
    )
```

```python
import math

import jax
import jax.numpy as jnp
from jax import lax
from jax.experimental import pallas as pl
from jax.experimental.pallas import tpu as pltpu
from jax.sharding import PartitionSpec as P

ANISO_GAIN = 1.0
SOFTNESS_LEVEL = 4.0
PRIOR_MASS = 1.0
STABILITY_FLOOR = 1e-06
LOG2E = math.log2(math.e)
NT = (((1,), (1,)), ((), ()))
F32 = jnp.float32
BF16 = jnp.bfloat16
LANES = 128


def hadamard(order):
    i = lax.broadcasted_iota(jnp.int32, (order, order), 0)
    j = lax.broadcasted_iota(jnp.int32, (order, order), 1)
    both = jnp.bitwise_and(i, j)
    parity = jnp.zeros((order, order), jnp.int32)
    for shift in range(order.bit_length() - 1):
        parity = parity + jnp.bitwise_and(jnp.right_shift(both, shift), 1)
    return (1 - 2 * jnp.bitwise_and(parity, 1)).astype(F32).astype(BF16)


def identity(order):
    i = lax.broadcasted_iota(jnp.int32, (order, order), 0)
    j = lax.broadcasted_iota(jnp.int32, (order, order), 1)
    return (i == j).astype(F32).astype(BF16)


def prepare_codes(m, ct_ref, c_ref, cb_ref, caug_ref):
    ct = ct_ref[m]
    width, codes = ct.shape
    wide = ct.astype(F32)
    c_ref[m] = wide.T.astype(BF16)
    square = jnp.sum(wide * wide, axis=0, keepdims=True) * (LOG2E / SOFTNESS_LEVEL)
    cb_ref[m] = jnp.broadcast_to(square, (LANES, codes)).T
    caug_ref[m, 0:width, :] = ct
    row = lax.broadcasted_iota(jnp.int32, (width, codes), 0)
    caug_ref[m, width : 2 * width, :] = jnp.where(row == 0, 1.0, 0.0).astype(BF16)


def rotate_block(block, rows, x_ref, rt_ref, own_ref, energy, width):
    outer = x_ref.shape[0]
    inner = x_ref.shape[2]
    h = hadamard(inner)
    parts = [
        lax.dot_general(h, x_ref[b, pl.ds(pl.multiple_of(block * rows, rows), rows), :], NT, preferred_element_type=F32)
        for b in range(outer)
    ]
    span = 1
    while span < outer:
        for b in range(outer):
            if not b & span:
                low, high = parts[b], parts[b | span]
                parts[b], parts[b | span] = low + high, low - high
        span *= 2
    scale = 1.0 / math.sqrt(outer * inner)
    total = jnp.zeros((1, rows), F32)
    for b in range(outer):
        rounded = (parts[b] * scale).astype(BF16)
        rt_ref[b * inner : (b + 1) * inner, :] = rounded
        wide = rounded.astype(F32)
        own = jnp.sum((wide * wide).reshape(inner // width, width, rows), axis=1)
        own_ref[b * (inner // width) : (b + 1) * (inner // width), :] = own
        total = total + jnp.sum(own, axis=0, keepdims=True)
    subspaces = outer * inner // width
    return ANISO_GAIN * subspaces * energy / (total * total + STABILITY_FLOOR)


def score(m, k, rows, stretch, own_ref, rt_ref, c_ref, cb_ref, t_refs, top_refs):
    codes, width = c_ref.shape[1:]
    x = rt_ref[pl.ds(pl.multiple_of(m * width, width), width), :]
    a = (1.0 + stretch * own_ref[pl.ds(m, 1), :]) * (2.0 * LOG2E / SOFTNESS_LEVEL)
    b = stretch * (LOG2E / SOFTNESS_LEVEL)
    g = jnp.dot(c_ref[m], x, preferred_element_type=F32)
    t = g * (a - b * g) - jnp.concatenate([cb_ref[m]] * (rows // LANES), axis=1)
    t_refs[k % 2][...] = t
    top_refs[k % 2][...] = jnp.max(t.reshape(codes // 8, 8, rows), axis=0)


def raise_scores(k, t_refs, top_refs, e_refs):
    top = jnp.max(top_refs[k % 2][...], axis=0, keepdims=True)
    e_refs[k % 4][...] = jnp.exp2(t_refs[k % 2][...] - top).astype(BF16)


def decode(m, k, rt_ref, caug_ref, dt_ref, e_refs, left_refs):
    width = caug_ref.shape[1] // 2
    at = pl.ds(pl.multiple_of(m * width, width), width)
    o = jnp.dot(caug_ref[m], e_refs[k % 4][...], preferred_element_type=F32)
    inv = 1.0 / o[width : width + 1, :]
    dt_ref[at, :] = (o[0:width, :] * inv).astype(BF16)
    row = lax.broadcasted_iota(jnp.int32, (width, o.shape[1]), 0)
    high = inv.astype(BF16).astype(F32)
    tail = jnp.where(row == 0, high, jnp.where(row == 1, inv - high, 0.0))
    left_refs[k % 2][...] = jnp.concatenate([rt_ref[at, :].astype(F32) * inv, tail], axis=0).astype(BF16)


def accumulate(m, k, sums_ref, e_refs, left_refs):
    width = left_refs[0].shape[0] // 2
    s = lax.dot_general(left_refs[k % 2][...], e_refs[k % 4][...], NT, preferred_element_type=F32)
    s = jnp.concatenate(
        [s[0:width], s[width : width + 1] + s[width + 1 : width + 2], s[width + 1 : width + 8]], axis=0
    )
    sums_ref[m] = sums_ref[m] + s


MESH = pl.DeviceIdType.MESH
SPAN = 16
SIDE = 4


def wait_bytes(ref, sem):
    pltpu.make_async_copy(ref, ref, sem).wait()


def remote(src, dst, there, send_sem, recv_sem):
    return pltpu.make_async_remote_copy(
        src_ref=src, dst_ref=dst, send_sem=send_sem, recv_sem=recv_sem, device_id=there, device_id_type=MESH
    )


def kernel(
    emb_hbm, sign_ref, order_hbm, ct_hbm, out_ref, new_ref,
    emb_ref, order_ref, ct_ref, wide, send, x_ref,
    part, part_rows, got_dims, got_rows,
    c_ref, cb_ref, caug_ref, rt_ref, own_ref, dt_ref, sums_ref,
    t_0, t_1, e_0, e_1, e_2, e_3, left_0, left_1, top_0, top_1,
    low, counts, got_low, got_counts, both, got_both, all_ref,
    load_sem, emb_sem, send_sem, recv_sem, esend_dims, erecv_dims, esend_rows, erecv_rows,
    sem_a, sem_b, sem_c, sem_d, sem_e, sem_f, sem_g, sem_h, sem_i, sem_j,
):
    r, d = lax.axis_index("rows"), lax.axis_index("dims")
    n_rows, n_dims = lax.axis_size("rows"), lax.axis_size("dims")
    devices, piece, inner = send.shape
    block = emb_ref.shape[0]
    subspaces, width, codes = ct_ref.shape
    outer, all_rows, _ = x_ref.shape
    rows = rt_ref.shape[1]
    blocks = all_rows // rows
    per_block = rows // piece
    group = subspaces // n_dims
    half = codes * group // n_rows
    halves = codes // half
    chunks = emb_sem.shape[0]
    chunk = block // chunks

    order_load = pltpu.make_async_copy(order_hbm, order_ref, load_sem.at[0])
    ct_load = pltpu.make_async_copy(ct_hbm, ct_ref, load_sem.at[1])

    def emb_load(i):
        at = pl.ds(pl.multiple_of(i * chunk, chunk), chunk)
        return pltpu.make_async_copy(emb_hbm.at[at], emb_ref.at[at], emb_sem.at[i])

    for i in range(chunks):
        emb_load(i).start()
    order_load.start()
    ct_load.start()

    barrier = pltpu.get_barrier_semaphore()

    def greet(j, low_k):
        for k in range(low_k, n_dims):
            there = (lax.rem(r + j, n_rows), lax.rem(d + k, n_dims))
            pl.semaphore_signal(barrier, inc=1, device_id=there, device_id_type=MESH)
        return low_k

    greet(0, 1)
    lax.fori_loop(1, n_rows, lambda j, carry: greet(j, 0) + carry, 0)

    sign = sign_ref[...].astype(F32)

    def widen(i, acc):
        emb_load(i).wait()
        step = 256
        for h in range(chunk // step):
            at = pl.ds(pl.multiple_of(i * chunk + h * step, step), step)
            v = emb_ref[at, :].astype(F32)
            wide[at, :] = v * sign
            acc = acc + jnp.sum((v * v).reshape(step // 8, 8, inner), axis=0)
        return acc

    part[...] = lax.fori_loop(0, chunks, widen, jnp.zeros((8, inner), F32))
    order_load.wait()

    def target(s, i, k):
        to_z = lax.rem(r // SIDE + i, SIDE)
        to_x = lax.rem(r + s + SIDE - i, SIDE)
        return to_z * SIDE + to_x, lax.rem(d + k + 2 * i, n_dims)

    def slot(s, i):
        return pl.ds(pl.multiple_of((s * per_block + i) * piece, piece), piece)

    def gather(s, i, k):
        to_r, to_d = target(s, i, k)
        q = to_r * n_dims + to_d
        first = q * piece
        for v in range(0, piece, 16):
            got = [wide[pl.ds(order_ref[first + v + u], 1), :] for u in range(16)]
            send[q, v : v + 16, :] = jnp.concatenate(got, axis=0).astype(BF16)

    def issue(s, i, k):
        to_r, to_d = target(s, i, k)
        q = to_r * n_dims + to_d
        remote(send.at[q], x_ref.at[d, slot(s, i), :], (to_r, to_d), send_sem.at[s], recv_sem.at[s]).start()

    def across(s, low_k, *steps):
        def step(k, carry):
            for one in steps:
                for i in range(per_block):
                    one(s, i, k)
            return carry

        lax.fori_loop(low_k, n_dims, step, 0)

    across(0, 0, gather)
    across(1, 0, gather)
    pl.semaphore_wait(barrier, devices - 1)

    for k in range(1, n_dims):
        there = (r, lax.rem(d + k, n_dims))
        remote(part, got_dims.at[k], there, esend_dims.at[k], erecv_dims.at[k]).start()
    pltpu.make_async_copy(send.at[r * n_dims + d], x_ref.at[d, slot(0, 0), :], recv_sem.at[0]).start()
    for i in range(1, per_block):
        issue(0, i, 0)
    across(0, 1, issue)

    ct_load.wait()

    def prep(i, carry):
        for k in range(8):
            prepare_codes(i * 8 + k, ct_ref, c_ref, cb_ref, caug_ref)
            sums_ref[i * 8 + k] = jnp.zeros(sums_ref.shape[1:], F32)
        return carry

    lax.fori_loop(0, subspaces // 8, prep, 0)
    across(1, 0, issue)

    total = part[...]
    for k in range(1, n_dims):
        wait_bytes(part, erecv_dims.at[k])
        total = total + got_dims[k]
    part_rows[...] = total
    for k in range(1, n_rows):
        there = (lax.rem(r + k, n_rows), d)
        remote(part_rows, got_rows.at[k], there, esend_rows.at[k], erecv_rows.at[k]).start()
    across(2, 0, gather, issue)
    for k in range(1, n_rows):
        wait_bytes(part, erecv_rows.at[k])
        total = total + got_rows[k]
    energy = jnp.sum(total, keepdims=True) / (block * n_rows)

    cores = 2
    ys = n_dims // cores
    y, core = d // cores, lax.rem(d, cores)

    def chunk_at(k):
        return lax.rem(y + k // cores, ys) * cores + lax.rem(core + lax.rem(k, cores), cores)

    def group_sums(k):
        there = chunk_at(k)
        at = pl.ds(pl.multiple_of(there * group, group), group)
        to = (r, there)
        return (
            remote(low.at[at], got_low.at[k], to, sem_a.at[k], sem_b.at[k]),
            remote(counts.at[at], got_counts.at[k], to, sem_c.at[k], sem_d.at[k]),
        )

    def send_sums(k):
        for g in range(group):
            m = chunk_at(k) * group + g
            low[m] = sums_ref[m, 0:width, :].astype(BF16)
            counts[pl.ds(m, 1), :] = sums_ref[m, width : width + 1, :]
        for copy in group_sums(k):
            copy.start()

    t_refs, e_refs = (t_0, t_1), (e_0, e_1, e_2, e_3)
    left_refs, top_refs = (left_0, left_1), (top_0, top_1)
    spans = subspaces // SPAN

    def flip(s):
        eye = identity(rows)
        for b in range(outer):
            lanes = slice(b * inner, (b + 1) * inner)
            flipped = lax.dot_general(eye, dt_ref[lanes, :], NT, preferred_element_type=F32).astype(BF16)
            for i in range(per_block):
                from_z = lax.rem(r // SIDE + SIDE - i, SIDE)
                from_x = lax.rem(r + 2 * SIDE - s + i, SIDE)
                at = pl.ds(pl.multiple_of((from_z * SIDE + from_x) * piece, piece), piece)
                out_ref[at, lanes] = flipped[i * piece : (i + 1) * piece]

    def one_block(s, carry):
        @pl.when(s == 1)
        def _():
            across(3, 0, gather, issue)

        wait_bytes(x_ref.at[:, pl.ds(pl.multiple_of(s * rows, rows), rows), :], recv_sem.at[s])
        stretch = rotate_block(s, rows, x_ref, rt_ref, own_ref, energy, width)

        def at_step(span, k):
            ahead = k // SPAN
            return lax.rem(y + 1 + span + ahead + spans, spans) * SPAN + k - ahead * SPAN

        def start(span, k):
            score(at_step(span, k), k, rows, stretch, own_ref, rt_ref, c_ref, cb_ref, t_refs, top_refs)

        def one_span(span, carry):
            for k in range(SPAN):
                start(span, k + 1)
                decode(at_step(span, k - 1), k - 1, rt_ref, caug_ref, dt_ref, e_refs, left_refs)
                m = at_step(span, k - 2)
                if k < 2:
                    m = jnp.where(span == 0, subspaces, m)
                accumulate(m, k - 2, sums_ref, e_refs, left_refs)
                raise_scores(k, t_refs, top_refs, e_refs)

            @pl.when(jnp.logical_and(s == blocks - 1, span > 0))
            def _():
                for c in range(cores):
                    send_sums(span * cores + c)

            return carry

        start(0, 0)
        lax.fori_loop(0, spans, one_span, 0)
        last = at_step(spans - 1, SPAN - 1)
        decode(last, SPAN - 1, rt_ref, caug_ref, dt_ref, e_refs, left_refs)
        accumulate(last - 1, SPAN - 2, sums_ref, e_refs, left_refs)
        accumulate(last, SPAN - 1, sums_ref, e_refs, left_refs)

        @pl.when(s < blocks - 1)
        def _():
            flip(s)

        return carry

    lax.fori_loop(0, blocks, one_block, 0)
    for k in range(1, cores):
        send_sums(k)

    sent = []

    def go(*args):
        copy = remote(*args)
        copy.start()
        sent.append(copy)

    mine = pl.ds(pl.multiple_of(d * group, group), group)
    total = sums_ref[mine, 0:width, :]
    total_counts = sums_ref[mine, width, :]
    for k in range(1, n_dims):
        wait_bytes(got_low.at[k], sem_b.at[k])
        wait_bytes(got_counts.at[k], sem_d.at[k])
        total = total + got_low[k].astype(F32)
        total_counts = total_counts + got_counts[k]
    for g in range(group):
        for h in range(halves):
            lanes = slice(h * half, (h + 1) * half)
            both[g * halves + h, 0:width, :] = total[g, :, lanes]
            both[g * halves + h, width : width + 8, :] = jnp.broadcast_to(total_counts[g : g + 1, lanes], (8, half))
    for k in range(1, n_rows):
        there = lax.rem(r + k, n_rows)
        go(both.at[there], got_both.at[k], (there, d), sem_e.at[k], sem_f.at[k])
    flip(blocks - 1)
    total = both[r]
    for k in range(1, n_rows):
        wait_bytes(got_both.at[k], sem_f.at[k])
        total = total + got_both[k]

    own_g = d * group + r // halves
    own_lanes = pl.ds(pl.multiple_of(lax.rem(r, halves) * half, half), half)
    new = (total[0:width] + PRIOR_MASS * ct_ref[own_g, :, own_lanes].astype(F32)) / (
        total[width : width + 1] + PRIOR_MASS
    )
    all_ref[d, r] = new.astype(BF16)
    for k in range(1, n_rows):
        there = lax.rem(r + k, n_rows)
        go(all_ref.at[d, r], all_ref.at[d, r], (there, d), sem_g.at[k], sem_h.at[k])
    for k in range(1, n_rows):
        wait_bytes(all_ref.at[d, lax.rem(r + n_rows - k, n_rows)], sem_h.at[k])
    partner = (r, y * cores + 1 - core)
    for k in range(1, ys):
        go(all_ref.at[d], all_ref.at[d], (r, lax.rem(y + k, ys) * cores + core), sem_i.at[k], sem_j.at[k])
    go(all_ref.at[d], all_ref.at[d], partner, sem_i.at[ys], sem_j.at[ys])

    def publish(e):
        for g in range(group):
            for h in range(halves):
                new_ref[e * group + g, :, h * half : (h + 1) * half] = all_ref[e, g * halves + h].astype(F32)

    publish(d)
    for k in range(1, ys):
        e = lax.rem(y + ys - k, ys) * cores + core
        wait_bytes(all_ref.at[e], sem_j.at[k])
        go(all_ref.at[e], all_ref.at[e], partner, sem_i.at[ys + k], sem_j.at[ys + k])
        publish(e)
    for k in range(ys):
        e = lax.rem(y + ys - k, ys) * cores + 1 - core
        wait_bytes(all_ref.at[e], sem_j.at[ys + k])
        publish(e)

    for copy in sent:
        copy.wait_send()
    for k in range(1, n_dims):
        for copy in group_sums(k):
            copy.wait_send()
        wait_bytes(part, esend_dims.at[k])
    for k in range(1, n_rows):
        wait_bytes(part, esend_rows.at[k])
    for s in range(blocks):
        wait_bytes(send.at[pl.ds(0, per_block * n_dims - (s == 0))], send_sem.at[s])


def body(embeddings, sign_flips, row_order, codebook):
    ct = codebook.transpose(0, 2, 1)
    n_rows, n_dims = lax.axis_size("rows"), lax.axis_size("dims")
    block, inner = embeddings.shape
    devices = n_rows * n_dims
    piece = block // devices
    subspaces, width, codes = ct.shape
    all_rows = block // n_dims
    rows = 256
    blocks = all_rows // rows
    group = subspaces // n_dims
    half = codes * group // n_rows
    full = n_dims * inner
    vmem = pl.BlockSpec(memory_space=pltpu.VMEM)
    hbm = pl.BlockSpec(memory_space=pl.ANY)
    dma = pltpu.SemaphoreType.DMA
    decoded, new = pl.pallas_call(
        kernel,
        out_shape=(
            pltpu.VMEM((all_rows, full), BF16),
            pltpu.VMEM((subspaces, width, codes), F32),
        ),
        in_specs=[hbm, vmem, hbm, hbm],
        out_specs=(vmem, vmem),
        scratch_shapes=[
            pltpu.VMEM((block, inner), BF16),
            pltpu.SMEM((block,), jnp.int32),
            pltpu.VMEM((subspaces, width, codes), BF16),
            pltpu.VMEM((block, inner), F32),
            pltpu.VMEM((devices, piece, inner), BF16),
            pltpu.VMEM((n_dims, all_rows, inner), BF16),
            pltpu.VMEM((8, inner), F32),
            pltpu.VMEM((8, inner), F32),
            pltpu.VMEM((n_dims, 8, inner), F32),
            pltpu.VMEM((n_rows, 8, inner), F32),
            pltpu.VMEM((subspaces, codes, width), BF16),
            pltpu.VMEM((subspaces, codes, LANES), F32),
            pltpu.VMEM((subspaces, 2 * width, codes), BF16),
            pltpu.VMEM((full, rows), BF16),
            pltpu.VMEM((subspaces, rows), F32),
            pltpu.VMEM((full, rows), BF16),
            pltpu.VMEM((subspaces + 1, width + 8, codes), F32),
        ]
        + [pltpu.VMEM((codes, rows), F32)] * 2
        + [pltpu.VMEM((codes, rows), BF16)] * 4
        + [pltpu.VMEM((2 * width, rows), BF16)] * 2
        + [pltpu.VMEM((8, rows), F32)] * 2
        + [
            pltpu.VMEM((subspaces, width, codes), BF16),
            pltpu.VMEM((subspaces, codes), F32),
            pltpu.VMEM((n_dims, group, width, codes), BF16),
            pltpu.VMEM((n_dims, group, codes), F32),
            pltpu.VMEM((n_rows, width + 8, half), F32),
            pltpu.VMEM((n_rows, width + 8, half), F32),
            pltpu.VMEM((n_dims, n_rows, width, half), BF16),
            dma((2,)),
            dma((8,)),
            dma((blocks,)),
            dma((blocks,)),
        ]
        + [dma((n_dims,))] * 2
        + [dma((n_rows,))] * 2
        + [dma((n_dims,))] * 4
        + [dma((n_rows,))] * 4
        + [dma((n_dims,))] * 2,
        compiler_params=pltpu.CompilerParams(
            collective_id=0, has_side_effects=True, vmem_limit_bytes=56 * 1024 * 1024
        ),
        name="update_codes",
    )(embeddings, sign_flips.reshape(1, inner), row_order, ct)
    return decoded, new.transpose(0, 2, 1)


def solution(mesh):
    return jax.shard_map(
        body,
        mesh=mesh,
        in_specs=(P("rows", "dims"), P("dims"), P("rows"), P()),
        out_specs=(P(("rows", "dims"), None), P()),
        check_vma=False,
    )
```

```python
import math

import jax
import jax.numpy as jnp
from jax import lax
from jax.experimental import pallas as pl
from jax.experimental.pallas import tpu as pltpu
from jax.sharding import PartitionSpec as P

ANISO_GAIN = 1.0
SOFTNESS_LEVEL = 4.0
PRIOR_MASS = 1.0
STABILITY_FLOOR = 1e-06
LOG2E = math.log2(math.e)
NT = (((1,), (1,)), ((), ()))
F32 = jnp.float32
BF16 = jnp.bfloat16
LANES = 128


def hadamard(order):
    i = lax.broadcasted_iota(jnp.int32, (order, order), 0)
    j = lax.broadcasted_iota(jnp.int32, (order, order), 1)
    both = jnp.bitwise_and(i, j)
    parity = jnp.zeros((order, order), jnp.int32)
    for shift in range(order.bit_length() - 1):
        parity = parity + jnp.bitwise_and(jnp.right_shift(both, shift), 1)
    return (1 - 2 * jnp.bitwise_and(parity, 1)).astype(F32).astype(BF16)


def identity(order):
    i = lax.broadcasted_iota(jnp.int32, (order, order), 0)
    j = lax.broadcasted_iota(jnp.int32, (order, order), 1)
    return (i == j).astype(F32).astype(BF16)


def prepare_codes(m, ct_ref, c_ref, cb_ref, caug_ref):
    ct = ct_ref[m]
    width, codes = ct.shape
    wide = ct.astype(F32)
    c_ref[m] = wide.T.astype(BF16)
    square = jnp.sum(wide * wide, axis=0, keepdims=True) * (LOG2E / SOFTNESS_LEVEL)
    cb_ref[m] = jnp.broadcast_to(square, (LANES, codes)).T
    caug_ref[m, 0:width, :] = ct
    row = lax.broadcasted_iota(jnp.int32, (width, codes), 0)
    caug_ref[m, width : 2 * width, :] = jnp.where(row == 0, 1.0, 0.0).astype(BF16)


def rotate_block(block, rows, x_ref, rt_ref, own_ref, width):
    outer = x_ref.shape[0]
    inner = x_ref.shape[2]
    h = hadamard(inner)
    parts = [
        lax.dot_general(h, x_ref[b, pl.ds(pl.multiple_of(block * rows, rows), rows), :], NT, preferred_element_type=F32)
        for b in range(outer)
    ]
    span = 1
    while span < outer:
        for b in range(outer):
            if not b & span:
                low, high = parts[b], parts[b | span]
                parts[b], parts[b | span] = low + high, low - high
        span *= 2
    scale = 1.0 / math.sqrt(outer * inner)
    total = jnp.zeros((1, rows), F32)
    for b in range(outer):
        rounded = (parts[b] * scale).astype(BF16)
        rt_ref[b * inner : (b + 1) * inner, :] = rounded
        wide = rounded.astype(F32)
        own = jnp.sum((wide * wide).reshape(inner // width, width, rows), axis=1)
        own_ref[b * (inner // width) : (b + 1) * (inner // width), :] = own
        total = total + jnp.sum(own, axis=0, keepdims=True)
    return total


def score(m, k, rows, stretch, own_ref, rt_ref, c_ref, cb_ref, t_refs, top_refs):
    codes, width = c_ref.shape[1:]
    x = rt_ref[pl.ds(pl.multiple_of(m * width, width), width), :]
    a = (1.0 + stretch * own_ref[pl.ds(m, 1), :]) * (2.0 * LOG2E / SOFTNESS_LEVEL)
    b = stretch * (LOG2E / SOFTNESS_LEVEL)
    g = jnp.dot(c_ref[m], x, preferred_element_type=F32)
    t = g * (a - b * g) - jnp.concatenate([cb_ref[m]] * (rows // LANES), axis=1)
    t_refs[k % 2][...] = t
    top_refs[k % 2][...] = jnp.max(t.reshape(codes // 8, 8, rows), axis=0)


def raise_scores(k, t_refs, top_refs, e_refs):
    top = jnp.max(top_refs[k % 2][...], axis=0, keepdims=True)
    e_refs[k % 4][...] = jnp.exp2(t_refs[k % 2][...] - top).astype(BF16)


def decode(m, k, rt_ref, caug_ref, dt_ref, e_refs, left_refs):
    width = caug_ref.shape[1] // 2
    at = pl.ds(pl.multiple_of(m * width, width), width)
    o = jnp.dot(caug_ref[m], e_refs[k % 4][...], preferred_element_type=F32)
    inv = 1.0 / o[width : width + 1, :]
    dt_ref[at, :] = (o[0:width, :] * inv).astype(BF16)
    row = lax.broadcasted_iota(jnp.int32, (width, o.shape[1]), 0)
    high = inv.astype(BF16).astype(F32)
    tail = jnp.where(row == 0, high, jnp.where(row == 1, inv - high, 0.0))
    left_refs[k % 2][...] = jnp.concatenate([rt_ref[at, :].astype(F32) * inv, tail], axis=0).astype(BF16)


def accumulate(m, k, sums_ref, e_refs, left_refs):
    width = left_refs[0].shape[0] // 2
    s = lax.dot_general(left_refs[k % 2][...], e_refs[k % 4][...], NT, preferred_element_type=F32)
    s = jnp.concatenate(
        [s[0:width], s[width : width + 1] + s[width + 1 : width + 2], s[width + 1 : width + 8]], axis=0
    )
    sums_ref[m] = sums_ref[m] + s


MESH = pl.DeviceIdType.MESH
SPAN = 16
SIDE = 4


def wait_bytes(ref, sem):
    pltpu.make_async_copy(ref, ref, sem).wait()


def remote(src, dst, there, send_sem, recv_sem):
    return pltpu.make_async_remote_copy(
        src_ref=src, dst_ref=dst, send_sem=send_sem, recv_sem=recv_sem, device_id=there, device_id_type=MESH
    )


def kernel(
    emb_hbm, sign_ref, order_hbm, ct_hbm, out_ref, new_ref,
    emb_ref, order_ref, ct_ref, wide, send, x_ref,
    part, part_rows, energy_ref, got_dims, got_rows,
    c_ref, cb_ref, caug_ref, rt_ref, own_ref, dt_ref, sums_ref,
    t_0, t_1, e_0, e_1, e_2, e_3, left_0, left_1, top_0, top_1,
    low, counts, got_low, got_counts, both, got_both, all_ref,
    load_sem, emb_sem, send_sem, recv_sem, esend_dims, erecv_dims, esend_rows, erecv_rows,
    sem_a, sem_b, sem_c, sem_d, sem_e, sem_f, sem_g, sem_h, sem_i, sem_j,
):
    r, d = lax.axis_index("rows"), lax.axis_index("dims")
    n_rows, n_dims = lax.axis_size("rows"), lax.axis_size("dims")
    devices, piece, inner = send.shape
    block = emb_ref.shape[0]
    subspaces, width, codes = ct_ref.shape
    outer, all_rows, _ = x_ref.shape
    rows = rt_ref.shape[1]
    blocks = all_rows // rows
    per_block = rows // piece
    group = subspaces // n_dims
    half = codes * group // n_rows
    halves = codes // half
    chunks = emb_sem.shape[0]
    chunk = block // chunks

    order_load = pltpu.make_async_copy(order_hbm, order_ref, load_sem.at[0])
    ct_load = pltpu.make_async_copy(ct_hbm, ct_ref, load_sem.at[1])

    def emb_load(i):
        at = pl.ds(pl.multiple_of(i * chunk, chunk), chunk)
        return pltpu.make_async_copy(emb_hbm.at[at], emb_ref.at[at], emb_sem.at[i])

    for i in range(chunks):
        emb_load(i).start()
    order_load.start()
    ct_load.start()

    barrier = pltpu.get_barrier_semaphore()

    to_dims = [lax.rem(d + k, n_dims) for k in range(n_dims)]
    to_zs = [lax.rem(r // SIDE + i, SIDE) * SIDE for i in range(SIDE)]
    to_xs = [lax.rem(r + i, SIDE) for i in range(SIDE)]

    def hops(step):
        return sum(min(i, SIDE - i) for i in (step[0], step[1], step[2] // 2))

    steps = [(i, j, k) for i in range(SIDE) for j in range(SIDE) for k in range(n_dims)]
    for i, j, k in sorted(steps, key=hops, reverse=True):
        if i or j or k:
            pl.semaphore_signal(barrier, inc=1, device_id=(to_zs[i] + to_xs[j], to_dims[k]), device_id_type=MESH)

    sign = sign_ref[...].astype(F32)

    def widen(i, acc):
        emb_load(i).wait()
        step = 256
        for h in range(chunk // step):
            at = pl.ds(pl.multiple_of(i * chunk + h * step, step), step)
            v = emb_ref[at, :].astype(F32)
            wide[at, :] = v * sign
            acc = acc + jnp.sum((v * v).reshape(step // 8, 8, inner), axis=0)
        return acc

    part[...] = lax.fori_loop(0, chunks, widen, jnp.zeros((8, inner), F32))
    order_load.wait()

    def target(s, i, k):
        to_r = to_zs[i] + lax.rem(r + s + SIDE - i, SIDE)
        if isinstance(k, int):
            return to_r, to_dims[(k + 2 * i) % n_dims]
        return to_r, lax.rem(d + k + 2 * i, n_dims)

    def slot(s, i):
        return pl.ds(pl.multiple_of((s * per_block + i) * piece, piece), piece)

    def gather(s, i, k):
        to_r, to_d = target(s, i, k)
        q = to_r * n_dims + to_d
        first = q * piece
        for v in range(0, piece, 16):
            got = [wide[pl.ds(order_ref[first + v + u], 1), :] for u in range(16)]
            send[q, v : v + 16, :] = jnp.concatenate(got, axis=0).astype(BF16)

    def issue(s, i, k):
        to_r, to_d = target(s, i, k)
        q = to_r * n_dims + to_d
        remote(send.at[q], x_ref.at[d, slot(s, i), :], (to_r, to_d), send_sem.at[s], recv_sem.at[s]).start()

    def gather_block(s):
        def step(k, carry):
            for i in range(per_block):
                gather(s, i, k)
            return carry

        lax.fori_loop(0, n_dims, step, 0)

    def issue_block(s, first, last):
        for n in range(first, last):
            issue(s, n % per_block, n // per_block)

    for b in range(blocks):
        gather_block(b)
    pl.semaphore_wait(barrier, devices - 1)

    for k in range(1, n_dims):
        there = (r, to_dims[k])
        remote(part, got_dims.at[k], there, esend_dims.at[k], erecv_dims.at[k]).start()
    pltpu.make_async_copy(send.at[r * n_dims + d], x_ref.at[d, slot(0, 0), :], recv_sem.at[0]).start()
    issue_block(0, 1, n_dims * per_block)

    total = part[...]
    for k in range(1, n_dims):
        wait_bytes(part, erecv_dims.at[k])
        total = total + got_dims[k]
    part_rows[...] = total
    for k in range(1, n_rows):
        there = (lax.rem(r + k, n_rows), d)
        remote(part_rows, got_rows.at[k], there, esend_rows.at[k], erecv_rows.at[k]).start()
    ct_load.wait()

    def prep(i, carry):
        for k in range(8):
            prepare_codes(i * 8 + k, ct_ref, c_ref, cb_ref, caug_ref)
            sums_ref[i * 8 + k] = jnp.zeros(sums_ref.shape[1:], F32)
        return carry

    lax.fori_loop(0, subspaces // 8, prep, 0)
    wait_bytes(send.at[pl.ds(0, per_block * n_dims - 1)], send_sem.at[0])
    issue_block(1, 0, n_dims * per_block)

    cores = 2
    ys = n_dims // cores
    y, core = d // cores, lax.rem(d, cores)

    def chunk_at(k):
        return lax.rem(y + k // cores, ys) * cores + lax.rem(core + lax.rem(k, cores), cores)

    def group_sums(k):
        there = chunk_at(k)
        at = pl.ds(pl.multiple_of(there * group, group), group)
        to = (r, there)
        return (
            remote(low.at[at], got_low.at[k], to, sem_a.at[k], sem_b.at[k]),
            remote(counts.at[at], got_counts.at[k], to, sem_c.at[k], sem_d.at[k]),
        )

    def send_sums(k):
        for g in range(group):
            m = chunk_at(k) * group + g
            low[m] = sums_ref[m, 0:width, :].astype(BF16)
            counts[pl.ds(m, 1), :] = sums_ref[m, width : width + 1, :]
        for copy in group_sums(k):
            copy.start()

    t_refs, e_refs = (t_0, t_1), (e_0, e_1, e_2, e_3)
    left_refs, top_refs = (left_0, left_1), (top_0, top_1)
    spans = subspaces // SPAN

    def flip(s):
        eye = identity(rows)
        for b in range(outer):
            lanes = slice(b * inner, (b + 1) * inner)
            flipped = lax.dot_general(eye, dt_ref[lanes, :], NT, preferred_element_type=F32).astype(BF16)
            for i in range(per_block):
                from_z = lax.rem(r // SIDE + SIDE - i, SIDE)
                from_x = lax.rem(r + 2 * SIDE - s + i, SIDE)
                at = pl.ds(pl.multiple_of((from_z * SIDE + from_x) * piece, piece), piece)
                out_ref[at, lanes] = flipped[i * piece : (i + 1) * piece]

    def one_block(s, carry):
        wait_bytes(x_ref.at[:, pl.ds(pl.multiple_of(s * rows, rows), rows), :], recv_sem.at[s])
        norms = rotate_block(s, rows, x_ref, rt_ref, own_ref, width)

        @pl.when(s == 0)
        def _():
            total = part_rows[...]
            for k in range(1, n_rows):
                wait_bytes(part, erecv_rows.at[k])
                total = total + got_rows[k]
            energy_ref[...] = jnp.broadcast_to(jnp.sum(total, keepdims=True) / (block * n_rows), energy_ref.shape)

        stretch = ANISO_GAIN * subspaces * energy_ref[0:1, 0:1] / (norms * norms + STABILITY_FLOOR)

        def at_step(span, k):
            ahead = k // SPAN
            return lax.rem(y + 1 + span + ahead + spans, spans) * SPAN + k - ahead * SPAN

        def start(span, k):
            score(at_step(span, k), k, rows, stretch, own_ref, rt_ref, c_ref, cb_ref, t_refs, top_refs)

        def one_span(span, carry):
            for k in range(SPAN):
                start(span, k + 1)
                decode(at_step(span, k - 1), k - 1, rt_ref, caug_ref, dt_ref, e_refs, left_refs)
                m = at_step(span, k - 2)
                if k < 2:
                    m = jnp.where(span == 0, subspaces, m)
                accumulate(m, k - 2, sums_ref, e_refs, left_refs)
                raise_scores(k, t_refs, top_refs, e_refs)

            for late in range(2, blocks):
                for half_block in range(2):

                    @pl.when(jnp.logical_and(s == 0, span == (late - 2) * 2 + half_block))
                    def _():
                        count = n_dims * per_block // 2
                        issue_block(late, half_block * count, (half_block + 1) * count)

            @pl.when(jnp.logical_and(s == blocks - 1, span > 0))
            def _():
                for c in range(cores):
                    send_sums(span * cores + c)

            return carry

        start(0, 0)
        lax.fori_loop(0, spans, one_span, 0)
        last = at_step(spans - 1, SPAN - 1)
        decode(last, SPAN - 1, rt_ref, caug_ref, dt_ref, e_refs, left_refs)
        accumulate(last - 1, SPAN - 2, sums_ref, e_refs, left_refs)
        accumulate(last, SPAN - 1, sums_ref, e_refs, left_refs)

        @pl.when(s < blocks - 1)
        def _():
            flip(s)

        return carry

    lax.fori_loop(0, blocks, one_block, 0)
    for k in range(1, cores):
        send_sums(k)

    sent = []

    def go(*args):
        copy = remote(*args)
        copy.start()
        sent.append(copy)

    mine = pl.ds(pl.multiple_of(d * group, group), group)
    total = sums_ref[mine, 0:width, :]
    total_counts = sums_ref[mine, width, :]
    for k in range(1, n_dims):
        wait_bytes(got_low.at[k], sem_b.at[k])
        wait_bytes(got_counts.at[k], sem_d.at[k])
        total = total + got_low[k].astype(F32)
        total_counts = total_counts + got_counts[k]
    for g in range(group):
        for h in range(halves):
            lanes = slice(h * half, (h + 1) * half)
            both[g * halves + h, 0:width, :] = total[g, :, lanes]
            both[g * halves + h, width : width + 8, :] = jnp.broadcast_to(total_counts[g : g + 1, lanes], (8, half))
    for k in range(1, n_rows):
        there = lax.rem(r + k, n_rows)
        go(both.at[there], got_both.at[k], (there, d), sem_e.at[k], sem_f.at[k])
    flip(blocks - 1)
    total = both[r]
    for k in range(1, n_rows):
        wait_bytes(got_both.at[k], sem_f.at[k])
        total = total + got_both[k]

    own_g = d * group + r // halves
    own_lanes = pl.ds(pl.multiple_of(lax.rem(r, halves) * half, half), half)
    new = (total[0:width] + PRIOR_MASS * ct_ref[own_g, :, own_lanes].astype(F32)) / (
        total[width : width + 1] + PRIOR_MASS
    )
    all_ref[d, r] = new.astype(BF16)
    for k in range(1, n_rows):
        there = lax.rem(r + k, n_rows)
        go(all_ref.at[d, r], all_ref.at[d, r], (there, d), sem_g.at[k], sem_h.at[k])
    for k in range(1, n_rows):
        wait_bytes(all_ref.at[d, lax.rem(r + n_rows - k, n_rows)], sem_h.at[k])
    partner = (r, y * cores + 1 - core)
    for k in range(1, ys):
        go(all_ref.at[d], all_ref.at[d], (r, lax.rem(y + k, ys) * cores + core), sem_i.at[k], sem_j.at[k])
    go(all_ref.at[d], all_ref.at[d], partner, sem_i.at[ys], sem_j.at[ys])

    def publish(e):
        for g in range(group):
            for h in range(halves):
                new_ref[e * group + g, :, h * half : (h + 1) * half] = all_ref[e, g * halves + h].astype(F32)

    publish(d)
    for k in range(1, ys):
        e = lax.rem(y + ys - k, ys) * cores + core
        wait_bytes(all_ref.at[e], sem_j.at[k])
        go(all_ref.at[e], all_ref.at[e], partner, sem_i.at[ys + k], sem_j.at[ys + k])
        publish(e)
    for k in range(ys):
        e = lax.rem(y + ys - k, ys) * cores + 1 - core
        wait_bytes(all_ref.at[e], sem_j.at[ys + k])
        publish(e)

    for copy in sent:
        copy.wait_send()
    for k in range(1, n_dims):
        for copy in group_sums(k):
            copy.wait_send()
        wait_bytes(part, esend_dims.at[k])
    for k in range(1, n_rows):
        wait_bytes(part, esend_rows.at[k])
    for s in range(1, blocks):
        wait_bytes(send.at[pl.ds(0, per_block * n_dims)], send_sem.at[s])


def body(embeddings, sign_flips, row_order, codebook):
    ct = codebook.transpose(0, 2, 1)
    n_rows, n_dims = lax.axis_size("rows"), lax.axis_size("dims")
    block, inner = embeddings.shape
    devices = n_rows * n_dims
    piece = block // devices
    subspaces, width, codes = ct.shape
    all_rows = block // n_dims
    rows = 256
    blocks = all_rows // rows
    group = subspaces // n_dims
    half = codes * group // n_rows
    full = n_dims * inner
    vmem = pl.BlockSpec(memory_space=pltpu.VMEM)
    hbm = pl.BlockSpec(memory_space=pl.ANY)
    dma = pltpu.SemaphoreType.DMA
    decoded, new = pl.pallas_call(
        kernel,
        out_shape=(
            pltpu.VMEM((all_rows, full), BF16),
            pltpu.VMEM((subspaces, width, codes), F32),
        ),
        in_specs=[hbm, vmem, hbm, hbm],
        out_specs=(vmem, vmem),
        scratch_shapes=[
            pltpu.VMEM((block, inner), BF16),
            pltpu.SMEM((block,), jnp.int32),
            pltpu.VMEM((subspaces, width, codes), BF16),
            pltpu.VMEM((block, inner), F32),
            pltpu.VMEM((devices, piece, inner), BF16),
            pltpu.VMEM((n_dims, all_rows, inner), BF16),
            pltpu.VMEM((8, inner), F32),
            pltpu.VMEM((8, inner), F32),
            pltpu.VMEM((8, inner), F32),
            pltpu.VMEM((n_dims, 8, inner), F32),
            pltpu.VMEM((n_rows, 8, inner), F32),
            pltpu.VMEM((subspaces, codes, width), BF16),
            pltpu.VMEM((subspaces, codes, LANES), F32),
            pltpu.VMEM((subspaces, 2 * width, codes), BF16),
            pltpu.VMEM((full, rows), BF16),
            pltpu.VMEM((subspaces, rows), F32),
            pltpu.VMEM((full, rows), BF16),
            pltpu.VMEM((subspaces + 1, width + 8, codes), F32),
        ]
        + [pltpu.VMEM((codes, rows), F32)] * 2
        + [pltpu.VMEM((codes, rows), BF16)] * 4
        + [pltpu.VMEM((2 * width, rows), BF16)] * 2
        + [pltpu.VMEM((8, rows), F32)] * 2
        + [
            pltpu.VMEM((subspaces, width, codes), BF16),
            pltpu.VMEM((subspaces, codes), F32),
            pltpu.VMEM((n_dims, group, width, codes), BF16),
            pltpu.VMEM((n_dims, group, codes), F32),
            pltpu.VMEM((n_rows, width + 8, half), F32),
            pltpu.VMEM((n_rows, width + 8, half), F32),
            pltpu.VMEM((n_dims, n_rows, width, half), BF16),
            dma((2,)),
            dma((8,)),
            dma((blocks,)),
            dma((blocks,)),
        ]
        + [dma((n_dims,))] * 2
        + [dma((n_rows,))] * 2
        + [dma((n_dims,))] * 4
        + [dma((n_rows,))] * 4
        + [dma((n_dims,))] * 2,
        compiler_params=pltpu.CompilerParams(
            collective_id=0, has_side_effects=True, vmem_limit_bytes=56 * 1024 * 1024
        ),
        name="update_codes",
    )(embeddings, sign_flips.reshape(1, inner), row_order, ct)
    return decoded, new.transpose(0, 2, 1)


def solution(mesh):
    return jax.shard_map(
        body,
        mesh=mesh,
        in_specs=(P("rows", "dims"), P("dims"), P("rows"), P()),
        out_specs=(P(("rows", "dims"), None), P()),
        check_vma=False,
    )
```

```python
import math

import jax
import jax.numpy as jnp
from jax import lax
from jax.experimental import pallas as pl
from jax.experimental.pallas import tpu as pltpu
from jax.sharding import PartitionSpec as P

ANISO_GAIN = 1.0
SOFTNESS_LEVEL = 4.0
PRIOR_MASS = 1.0
STABILITY_FLOOR = 1e-06
LOG2E = math.log2(math.e)
NT = (((1,), (1,)), ((), ()))
F32 = jnp.float32
BF16 = jnp.bfloat16
LANES = 128


def hadamard(order):
    i = lax.broadcasted_iota(jnp.int32, (order, order), 0)
    j = lax.broadcasted_iota(jnp.int32, (order, order), 1)
    both = jnp.bitwise_and(i, j)
    parity = jnp.zeros((order, order), jnp.int32)
    for shift in range(order.bit_length() - 1):
        parity = parity + jnp.bitwise_and(jnp.right_shift(both, shift), 1)
    return (1 - 2 * jnp.bitwise_and(parity, 1)).astype(F32).astype(BF16)


def identity(order):
    i = lax.broadcasted_iota(jnp.int32, (order, order), 0)
    j = lax.broadcasted_iota(jnp.int32, (order, order), 1)
    return (i == j).astype(F32).astype(BF16)


def prepare_codes(m, ct_ref, c_ref, cb_ref, caug_ref):
    ct = ct_ref[m]
    width, codes = ct.shape
    wide = ct.astype(F32)
    c_ref[m] = wide.T.astype(BF16)
    square = jnp.sum(wide * wide, axis=0, keepdims=True) * (LOG2E / SOFTNESS_LEVEL)
    cb_ref[m] = jnp.broadcast_to(square, (LANES, codes)).T
    caug_ref[m, 0:width, :] = ct
    row = lax.broadcasted_iota(jnp.int32, (width, codes), 0)
    caug_ref[m, width : 2 * width, :] = jnp.where(row == 0, 1.0, 0.0).astype(BF16)


def rotate_block(block, rows, x_ref, rt_ref, own_ref, width):
    outer = x_ref.shape[0]
    inner = x_ref.shape[2]
    h = hadamard(inner)
    parts = [
        lax.dot_general(h, x_ref[b, pl.ds(pl.multiple_of(block * rows, rows), rows), :], NT, preferred_element_type=F32)
        for b in range(outer)
    ]
    span = 1
    while span < outer:
        for b in range(outer):
            if not b & span:
                low, high = parts[b], parts[b | span]
                parts[b], parts[b | span] = low + high, low - high
        span *= 2
    scale = 1.0 / math.sqrt(outer * inner)
    total = jnp.zeros((1, rows), F32)
    for b in range(outer):
        rounded = (parts[b] * scale).astype(BF16)
        rt_ref[b * inner : (b + 1) * inner, :] = rounded
        wide = rounded.astype(F32)
        own = jnp.sum((wide * wide).reshape(inner // width, width, rows), axis=1)
        own_ref[b * (inner // width) : (b + 1) * (inner // width), :] = own
        total = total + jnp.sum(own, axis=0, keepdims=True)
    return total


def score(m, k, rows, stretch, own_ref, rt_ref, c_ref, cb_ref, t_refs, top_refs):
    codes, width = c_ref.shape[1:]
    x = rt_ref[pl.ds(pl.multiple_of(m * width, width), width), :]
    a = (1.0 + stretch * own_ref[pl.ds(m, 1), :]) * (2.0 * LOG2E / SOFTNESS_LEVEL)
    b = stretch * (LOG2E / SOFTNESS_LEVEL)
    g = jnp.dot(c_ref[m], x, preferred_element_type=F32)
    t = g * (a - b * g) - jnp.concatenate([cb_ref[m]] * (rows // LANES), axis=1)
    t_refs[k % 2][...] = t
    top_refs[k % 2][...] = jnp.max(t.reshape(codes // 8, 8, rows), axis=0)


def raise_scores(k, t_refs, top_refs, e_refs):
    top = jnp.max(top_refs[k % 2][...], axis=0, keepdims=True)
    e_refs[k % 4][...] = jnp.exp2(t_refs[k % 2][...] - top).astype(BF16)


def decode(m, k, rt_ref, caug_ref, dt_ref, e_refs, left_refs):
    width = caug_ref.shape[1] // 2
    at = pl.ds(pl.multiple_of(m * width, width), width)
    o = jnp.dot(caug_ref[m], e_refs[k % 4][...], preferred_element_type=F32)
    inv = 1.0 / o[width : width + 1, :]
    dt_ref[at, :] = (o[0:width, :] * inv).astype(BF16)
    row = lax.broadcasted_iota(jnp.int32, (width, o.shape[1]), 0)
    high = inv.astype(BF16).astype(F32)
    tail = jnp.where(row == 0, high, jnp.where(row == 1, inv - high, 0.0))
    left_refs[k % 2][...] = jnp.concatenate([rt_ref[at, :].astype(F32) * inv, tail], axis=0).astype(BF16)


def accumulate(m, k, sums_ref, e_refs, left_refs):
    width = left_refs[0].shape[0] // 2
    s = lax.dot_general(left_refs[k % 2][...], e_refs[k % 4][...], NT, preferred_element_type=F32)
    s = jnp.concatenate(
        [s[0:width], s[width : width + 1] + s[width + 1 : width + 2], s[width + 1 : width + 8]], axis=0
    )
    sums_ref[m] = sums_ref[m] + s


MESH = pl.DeviceIdType.MESH
SPAN = 16
SIDE = 4


def wait_bytes(ref, sem):
    pltpu.make_async_copy(ref, ref, sem).wait()


def remote(src, dst, there, send_sem, recv_sem):
    return pltpu.make_async_remote_copy(
        src_ref=src, dst_ref=dst, send_sem=send_sem, recv_sem=recv_sem, device_id=there, device_id_type=MESH
    )


def kernel(
    emb_hbm, sign_ref, order_hbm, ct_hbm, out_ref, new_ref,
    emb_ref, order_ref, ct_ref, wide, send, x_ref,
    part, part_rows, energy_ref, got_dims, got_rows,
    c_ref, cb_ref, caug_ref, rt_ref, own_ref, dt_ref, sums_ref,
    t_0, t_1, e_0, e_1, e_2, e_3, left_0, left_1, top_0, top_1,
    low, counts, got_low, got_counts, both, got_both, all_ref,
    load_sem, emb_sem, send_sem, recv_sem, esend_dims, erecv_dims, esend_rows, erecv_rows,
    sem_a, sem_b, sem_c, sem_d, sem_e, sem_f, sem_g, sem_h, sem_i, sem_j,
):
    r, d = lax.axis_index("rows"), lax.axis_index("dims")
    n_rows, n_dims = lax.axis_size("rows"), lax.axis_size("dims")
    devices, piece, inner = send.shape
    block = emb_ref.shape[0]
    subspaces, width, codes = ct_ref.shape
    outer, all_rows, _ = x_ref.shape
    rows = rt_ref.shape[1]
    blocks = all_rows // rows
    per_block = rows // piece
    group = subspaces // n_dims
    half = codes * group // n_rows
    halves = codes // half
    chunks = emb_sem.shape[0]
    chunk = block // chunks

    order_load = pltpu.make_async_copy(order_hbm, order_ref, load_sem.at[0])
    ct_load = pltpu.make_async_copy(ct_hbm, ct_ref, load_sem.at[1])

    def emb_load(i):
        at = pl.ds(pl.multiple_of(i * chunk, chunk), chunk)
        return pltpu.make_async_copy(emb_hbm.at[at], emb_ref.at[at], emb_sem.at[i])

    for i in range(chunks):
        emb_load(i).start()
    order_load.start()
    ct_load.start()

    barrier = pltpu.get_barrier_semaphore()

    to_dims = [lax.rem(d + k, n_dims) for k in range(n_dims)]
    to_zs = [lax.rem(r // SIDE + i, SIDE) * SIDE for i in range(SIDE)]
    to_xs = [lax.rem(r + i, SIDE) for i in range(SIDE)]

    def hops(step):
        return sum(min(i, SIDE - i) for i in (step[0], step[1], step[2] // 2))

    steps = [(i, j, k) for i in range(SIDE) for j in range(SIDE) for k in range(n_dims)]
    for i, j, k in sorted(steps, key=hops, reverse=True):
        if i or j or k:
            pl.semaphore_signal(barrier, inc=1, device_id=(to_zs[i] + to_xs[j], to_dims[k]), device_id_type=MESH)

    sign = sign_ref[...].astype(F32)

    def widen(i, acc):
        emb_load(i).wait()
        step = 256
        for h in range(chunk // step):
            at = pl.ds(pl.multiple_of(i * chunk + h * step, step), step)
            v = emb_ref[at, :].astype(F32)
            wide[at, :] = v * sign
            acc = acc + jnp.sum((v * v).reshape(step // 8, 8, inner), axis=0)
        return acc

    part[...] = lax.fori_loop(0, chunks, widen, jnp.zeros((8, inner), F32))
    order_load.wait()

    def target(s, i, k):
        to_r = to_zs[i] + lax.rem(r + s + SIDE - i, SIDE)
        if isinstance(k, int):
            return to_r, to_dims[(k + 2 * i) % n_dims]
        return to_r, lax.rem(d + k + 2 * i, n_dims)

    def slot(s, i):
        return pl.ds(pl.multiple_of((s * per_block + i) * piece, piece), piece)

    def gather(s, i, k):
        to_r, to_d = target(s, i, k)
        q = to_r * n_dims + to_d
        first = q * piece
        for v in range(0, piece, 16):
            got = [wide[pl.ds(order_ref[first + v + u], 1), :] for u in range(16)]
            send[q, v : v + 16, :] = jnp.concatenate(got, axis=0).astype(BF16)

    def issue(s, i, k):
        to_r, to_d = target(s, i, k)
        q = to_r * n_dims + to_d
        remote(send.at[q], x_ref.at[d, slot(s, i), :], (to_r, to_d), send_sem.at[s], recv_sem.at[s]).start()

    def gather_block(s):
        def step(k, carry):
            for i in range(per_block):
                gather(s, i, k)
            return carry

        lax.fori_loop(0, n_dims, step, 0)

    def issue_block(s, first, last):
        for n in range(first, last):
            issue(s, n % per_block, n // per_block)

    for b in range(blocks):
        gather_block(b)
    pl.semaphore_wait(barrier, devices - 1)

    for k in range(1, n_dims):
        there = (r, to_dims[k])
        remote(part, got_dims.at[k], there, esend_dims.at[k], erecv_dims.at[k]).start()
    pltpu.make_async_copy(send.at[r * n_dims + d], x_ref.at[d, slot(0, 0), :], recv_sem.at[0]).start()
    issue_block(0, 1, n_dims * per_block)

    total = part[...]
    for k in range(1, n_dims):
        wait_bytes(part, erecv_dims.at[k])
        total = total + got_dims[k]
    part_rows[...] = total
    for k in range(1, n_rows):
        there = (lax.rem(r + k, n_rows), d)
        remote(part_rows, got_rows.at[k], there, esend_rows.at[k], erecv_rows.at[k]).start()
    ct_load.wait()

    def prep(i, carry):
        for k in range(8):
            prepare_codes(i * 8 + k, ct_ref, c_ref, cb_ref, caug_ref)
            sums_ref[i * 8 + k] = jnp.zeros(sums_ref.shape[1:], F32)
        return carry

    lax.fori_loop(0, subspaces // 8, prep, 0)
    wait_bytes(send.at[pl.ds(0, per_block * n_dims - 1)], send_sem.at[0])
    issue_block(1, 0, n_dims * per_block)

    cores = 2
    ys = n_dims // cores
    y, core = d // cores, lax.rem(d, cores)

    def chunk_at(k):
        return lax.rem(y + k // cores, ys) * cores + lax.rem(core + lax.rem(k, cores), cores)

    def group_sums(k):
        there = chunk_at(k)
        at = pl.ds(pl.multiple_of(there * group, group), group)
        to = (r, there)
        return (
            remote(low.at[at], got_low.at[k], to, sem_a.at[k], sem_b.at[k]),
            remote(counts.at[at], got_counts.at[k], to, sem_c.at[k], sem_d.at[k]),
        )

    def send_sums(k):
        for g in range(group):
            m = chunk_at(k) * group + g
            low[m] = sums_ref[m, 0:width, :].astype(BF16)
            counts[pl.ds(m, 1), :] = sums_ref[m, width : width + 1, :]
        for copy in group_sums(k):
            copy.start()

    def turn(span, h):
        dy = jnp.where(span == 0, 2, jnp.where(span == spans - 1, 0, 1 + 2 * h))
        dcore = jnp.where(span == 0, h, jnp.where(span == spans - 1, 1 - h, span - 1))
        return dy * cores + dcore

    t_refs, e_refs = (t_0, t_1), (e_0, e_1, e_2, e_3)
    left_refs, top_refs = (left_0, left_1), (top_0, top_1)
    spans = subspaces // SPAN

    def flip(s):
        eye = identity(rows)
        for b in range(outer):
            lanes = slice(b * inner, (b + 1) * inner)
            flipped = lax.dot_general(eye, dt_ref[lanes, :], NT, preferred_element_type=F32).astype(BF16)
            for i in range(per_block):
                from_z = lax.rem(r // SIDE + SIDE - i, SIDE)
                from_x = lax.rem(r + 2 * SIDE - s + i, SIDE)
                at = pl.ds(pl.multiple_of((from_z * SIDE + from_x) * piece, piece), piece)
                out_ref[at, lanes] = flipped[i * piece : (i + 1) * piece]

    def one_block(s, carry):
        wait_bytes(x_ref.at[:, pl.ds(pl.multiple_of(s * rows, rows), rows), :], recv_sem.at[s])
        norms = rotate_block(s, rows, x_ref, rt_ref, own_ref, width)

        @pl.when(s == 0)
        def _():
            total = part_rows[...]
            for k in range(1, n_rows):
                wait_bytes(part, erecv_rows.at[k])
                total = total + got_rows[k]
            energy_ref[...] = jnp.broadcast_to(jnp.sum(total, keepdims=True) / (block * n_rows), energy_ref.shape)

        stretch = ANISO_GAIN * subspaces * energy_ref[0:1, 0:1] / (norms * norms + STABILITY_FLOOR)

        def at_step(span, k):
            ahead, k = k // SPAN, k % SPAN
            return chunk_at(turn(lax.rem(span + ahead + spans, spans), k // group)) * group + k % group

        def start(span, k):
            score(at_step(span, k), k, rows, stretch, own_ref, rt_ref, c_ref, cb_ref, t_refs, top_refs)

        def drain(span):
            last = at_step(span, SPAN - 1)
            decode(last, SPAN - 1, rt_ref, caug_ref, dt_ref, e_refs, left_refs)
            accumulate(last - 1, SPAN - 2, sums_ref, e_refs, left_refs)
            accumulate(last, SPAN - 1, sums_ref, e_refs, left_refs)

        def one_span(span, carry):
            for k in range(SPAN):
                start(span, k + 1)
                decode(at_step(span, k - 1), k - 1, rt_ref, caug_ref, dt_ref, e_refs, left_refs)
                m = at_step(span, k - 2)
                if k < 2:
                    m = jnp.where(jnp.logical_or(span == 0, s == blocks - 1), subspaces, m)
                accumulate(m, k - 2, sums_ref, e_refs, left_refs)
                raise_scores(k, t_refs, top_refs, e_refs)

            for late in range(2, blocks):
                for half_block in range(2):

                    @pl.when(jnp.logical_and(s == 0, span == (late - 2) * 2 + half_block))
                    def _():
                        count = n_dims * per_block // 2
                        issue_block(late, half_block * count, (half_block + 1) * count)

            @pl.when(s == blocks - 1)
            def _():
                drain(span)

                @pl.when(span < spans - 1)
                def _():
                    for h in range(SPAN // group):
                        send_sums(turn(span, h))

            return carry

        start(0, 0)
        lax.fori_loop(0, spans, one_span, 0)

        @pl.when(s < blocks - 1)
        def _():
            drain(spans - 1)
            flip(s)

        return carry

    lax.fori_loop(0, blocks, one_block, 0)
    for k in range(1, cores):
        send_sums(k)

    sent = []

    def go(*args):
        copy = remote(*args)
        copy.start()
        sent.append(copy)

    mine = pl.ds(pl.multiple_of(d * group, group), group)
    total = sums_ref[mine, 0:width, :]
    total_counts = sums_ref[mine, width, :]
    for k in range(1, n_dims):
        wait_bytes(got_low.at[k], sem_b.at[k])
        wait_bytes(got_counts.at[k], sem_d.at[k])
        total = total + got_low[k].astype(F32)
        total_counts = total_counts + got_counts[k]
    for g in range(group):
        for h in range(halves):
            lanes = slice(h * half, (h + 1) * half)
            both[g * halves + h, 0:width, :] = total[g, :, lanes]
            both[g * halves + h, width : width + 8, :] = jnp.broadcast_to(total_counts[g : g + 1, lanes], (8, half))
    for k in range(1, n_rows):
        there = lax.rem(r + k, n_rows)
        go(both.at[there], got_both.at[k], (there, d), sem_e.at[k], sem_f.at[k])
    flip(blocks - 1)
    total = both[r]
    for k in range(1, n_rows):
        wait_bytes(got_both.at[k], sem_f.at[k])
        total = total + got_both[k]

    own_g = d * group + r // halves
    own_lanes = pl.ds(pl.multiple_of(lax.rem(r, halves) * half, half), half)
    new = (total[0:width] + PRIOR_MASS * ct_ref[own_g, :, own_lanes].astype(F32)) / (
        total[width : width + 1] + PRIOR_MASS
    )
    all_ref[d, r] = new.astype(BF16)
    for k in range(1, n_rows):
        there = lax.rem(r + k, n_rows)
        go(all_ref.at[d, r], all_ref.at[d, r], (there, d), sem_g.at[k], sem_h.at[k])
    for k in range(1, n_rows):
        wait_bytes(all_ref.at[d, lax.rem(r + n_rows - k, n_rows)], sem_h.at[k])
    partner = (r, y * cores + 1 - core)
    for k in range(1, ys):
        go(all_ref.at[d], all_ref.at[d], (r, lax.rem(y + k, ys) * cores + core), sem_i.at[k], sem_j.at[k])
    go(all_ref.at[d], all_ref.at[d], partner, sem_i.at[ys], sem_j.at[ys])

    def publish(e):
        for g in range(group):
            for h in range(halves):
                new_ref[e * group + g, :, h * half : (h + 1) * half] = all_ref[e, g * halves + h].astype(F32)

    publish(d)
    for k in range(1, ys):
        e = lax.rem(y + ys - k, ys) * cores + core
        wait_bytes(all_ref.at[e], sem_j.at[k])
        go(all_ref.at[e], all_ref.at[e], partner, sem_i.at[ys + k], sem_j.at[ys + k])
        publish(e)
    for k in range(ys):
        e = lax.rem(y + ys - k, ys) * cores + 1 - core
        wait_bytes(all_ref.at[e], sem_j.at[ys + k])
        publish(e)

    for copy in sent:
        copy.wait_send()
    for k in range(1, n_dims):
        for copy in group_sums(k):
            copy.wait_send()
        wait_bytes(part, esend_dims.at[k])
    for k in range(1, n_rows):
        wait_bytes(part, esend_rows.at[k])
    for s in range(1, blocks):
        wait_bytes(send.at[pl.ds(0, per_block * n_dims)], send_sem.at[s])


def body(embeddings, sign_flips, row_order, codebook):
    ct = codebook.transpose(0, 2, 1)
    n_rows, n_dims = lax.axis_size("rows"), lax.axis_size("dims")
    block, inner = embeddings.shape
    devices = n_rows * n_dims
    piece = block // devices
    subspaces, width, codes = ct.shape
    all_rows = block // n_dims
    rows = 256
    blocks = all_rows // rows
    group = subspaces // n_dims
    half = codes * group // n_rows
    full = n_dims * inner
    vmem = pl.BlockSpec(memory_space=pltpu.VMEM)
    hbm = pl.BlockSpec(memory_space=pl.ANY)
    dma = pltpu.SemaphoreType.DMA
    decoded, new = pl.pallas_call(
        kernel,
        out_shape=(
            pltpu.VMEM((all_rows, full), BF16),
            pltpu.VMEM((subspaces, width, codes), F32),
        ),
        in_specs=[hbm, vmem, hbm, hbm],
        out_specs=(vmem, vmem),
        scratch_shapes=[
            pltpu.VMEM((block, inner), BF16),
            pltpu.SMEM((block,), jnp.int32),
            pltpu.VMEM((subspaces, width, codes), BF16),
            pltpu.VMEM((block, inner), F32),
            pltpu.VMEM((devices, piece, inner), BF16),
            pltpu.VMEM((n_dims, all_rows, inner), BF16),
            pltpu.VMEM((8, inner), F32),
            pltpu.VMEM((8, inner), F32),
            pltpu.VMEM((8, inner), F32),
            pltpu.VMEM((n_dims, 8, inner), F32),
            pltpu.VMEM((n_rows, 8, inner), F32),
            pltpu.VMEM((subspaces, codes, width), BF16),
            pltpu.VMEM((subspaces, codes, LANES), F32),
            pltpu.VMEM((subspaces, 2 * width, codes), BF16),
            pltpu.VMEM((full, rows), BF16),
            pltpu.VMEM((subspaces, rows), F32),
            pltpu.VMEM((full, rows), BF16),
            pltpu.VMEM((subspaces + 1, width + 8, codes), F32),
        ]
        + [pltpu.VMEM((codes, rows), F32)] * 2
        + [pltpu.VMEM((codes, rows), BF16)] * 4
        + [pltpu.VMEM((2 * width, rows), BF16)] * 2
        + [pltpu.VMEM((8, rows), F32)] * 2
        + [
            pltpu.VMEM((subspaces, width, codes), BF16),
            pltpu.VMEM((subspaces, codes), F32),
            pltpu.VMEM((n_dims, group, width, codes), BF16),
            pltpu.VMEM((n_dims, group, codes), F32),
            pltpu.VMEM((n_rows, width + 8, half), F32),
            pltpu.VMEM((n_rows, width + 8, half), F32),
            pltpu.VMEM((n_dims, n_rows, width, half), BF16),
            dma((2,)),
            dma((8,)),
            dma((blocks,)),
            dma((blocks,)),
        ]
        + [dma((n_dims,))] * 2
        + [dma((n_rows,))] * 2
        + [dma((n_dims,))] * 4
        + [dma((n_rows,))] * 4
        + [dma((n_dims,))] * 2,
        compiler_params=pltpu.CompilerParams(
            collective_id=0, has_side_effects=True, vmem_limit_bytes=56 * 1024 * 1024
        ),
        name="update_codes",
    )(embeddings, sign_flips.reshape(1, inner), row_order, ct)
    return decoded, new.transpose(0, 2, 1)


def solution(mesh):
    return jax.shard_map(
        body,
        mesh=mesh,
        in_specs=(P("rows", "dims"), P("dims"), P("rows"), P()),
        out_specs=(P(("rows", "dims"), None), P()),
        check_vma=False,
    )
```

```python
import math

import jax
import jax.numpy as jnp
from jax import lax
from jax.experimental import pallas as pl
from jax.experimental.pallas import tpu as pltpu
from jax.sharding import PartitionSpec as P

ANISO_GAIN = 1.0
SOFTNESS_LEVEL = 4.0
PRIOR_MASS = 1.0
STABILITY_FLOOR = 1e-06
LOG2E = math.log2(math.e)
NT = (((1,), (1,)), ((), ()))
F32 = jnp.float32
BF16 = jnp.bfloat16
LANES = 128


def hadamard(order):
    i = lax.broadcasted_iota(jnp.int32, (order, order), 0)
    j = lax.broadcasted_iota(jnp.int32, (order, order), 1)
    both = jnp.bitwise_and(i, j)
    parity = jnp.zeros((order, order), jnp.int32)
    for shift in range(order.bit_length() - 1):
        parity = parity + jnp.bitwise_and(jnp.right_shift(both, shift), 1)
    return (1 - 2 * jnp.bitwise_and(parity, 1)).astype(F32).astype(BF16)


def identity(order):
    i = lax.broadcasted_iota(jnp.int32, (order, order), 0)
    j = lax.broadcasted_iota(jnp.int32, (order, order), 1)
    return (i == j).astype(F32).astype(BF16)


def prepare_codes(m, ct_ref, c_ref, cb_ref, caug_ref):
    ct = ct_ref[m]
    width, codes = ct.shape
    wide = ct.astype(F32)
    c_ref[m] = wide.T.astype(BF16)
    square = jnp.sum(wide * wide, axis=0, keepdims=True) * (LOG2E / SOFTNESS_LEVEL)
    cb_ref[m] = jnp.broadcast_to(square, (LANES, codes)).T
    caug_ref[m, 0:width, :] = ct
    row = lax.broadcasted_iota(jnp.int32, (width, codes), 0)
    caug_ref[m, width : 2 * width, :] = jnp.where(row == 0, 1.0, 0.0).astype(BF16)


def rotate_block(block, rows, x_ref, rt_ref, own_ref, width):
    outer = x_ref.shape[0]
    inner = x_ref.shape[2]
    h = hadamard(inner)
    parts = [
        lax.dot_general(h, x_ref[b, pl.ds(pl.multiple_of(block * rows, rows), rows), :], NT, preferred_element_type=F32)
        for b in range(outer)
    ]
    span = 1
    while span < outer:
        for b in range(outer):
            if not b & span:
                low, high = parts[b], parts[b | span]
                parts[b], parts[b | span] = low + high, low - high
        span *= 2
    scale = 1.0 / math.sqrt(outer * inner)
    total = jnp.zeros((1, rows), F32)
    for b in range(outer):
        rounded = (parts[b] * scale).astype(BF16)
        rt_ref[b * inner : (b + 1) * inner, :] = rounded
        wide = rounded.astype(F32)
        own = jnp.sum((wide * wide).reshape(inner // width, width, rows), axis=1)
        own_ref[b * (inner // width) : (b + 1) * (inner // width), :] = own
        total = total + jnp.sum(own, axis=0, keepdims=True)
    return total


def score(m, k, rows, stretch, own_ref, rt_ref, c_ref, cb_ref, t_refs, top_refs):
    codes, width = c_ref.shape[1:]
    x = rt_ref[pl.ds(pl.multiple_of(m * width, width), width), :]
    a = (1.0 + stretch * own_ref[pl.ds(m, 1), :]) * (2.0 * LOG2E / SOFTNESS_LEVEL)
    b = stretch * (LOG2E / SOFTNESS_LEVEL)
    g = jnp.dot(c_ref[m], x, preferred_element_type=F32)
    t = g * (a - b * g) - jnp.concatenate([cb_ref[m]] * (rows // LANES), axis=1)
    t_refs[k % 2][...] = t
    top_refs[k % 2][...] = jnp.max(t.reshape(codes // 8, 8, rows), axis=0)


def raise_scores(k, t_refs, top_refs, e_refs):
    top = jnp.max(top_refs[k % 2][...], axis=0, keepdims=True)
    e_refs[k % 4][...] = jnp.exp2(t_refs[k % 2][...] - top).astype(BF16)


def decode(m, k, rt_ref, caug_ref, dt_ref, e_refs, left_refs):
    width = caug_ref.shape[1] // 2
    at = pl.ds(pl.multiple_of(m * width, width), width)
    o = jnp.dot(caug_ref[m], e_refs[k % 4][...], preferred_element_type=F32)
    inv = 1.0 / o[width : width + 1, :]
    dt_ref[at, :] = (o[0:width, :] * inv).astype(BF16)
    row = lax.broadcasted_iota(jnp.int32, (width, o.shape[1]), 0)
    high = inv.astype(BF16).astype(F32)
    tail = jnp.where(row == 0, high, jnp.where(row == 1, inv - high, 0.0))
    left_refs[k % 2][...] = jnp.concatenate([rt_ref[at, :].astype(F32) * inv, tail], axis=0).astype(BF16)


def accumulate(m, k, sums_ref, e_refs, left_refs):
    width = left_refs[0].shape[0] // 2
    s = lax.dot_general(left_refs[k % 2][...], e_refs[k % 4][...], NT, preferred_element_type=F32)
    s = jnp.concatenate(
        [s[0:width], s[width : width + 1] + s[width + 1 : width + 2], s[width + 1 : width + 8]], axis=0
    )
    sums_ref[m] = sums_ref[m] + s


MESH = pl.DeviceIdType.MESH
SPAN = 16
SIDE = 4


def wait_bytes(ref, sem):
    pltpu.make_async_copy(ref, ref, sem).wait()


def remote(src, dst, there, send_sem, recv_sem):
    return pltpu.make_async_remote_copy(
        src_ref=src, dst_ref=dst, send_sem=send_sem, recv_sem=recv_sem, device_id=there, device_id_type=MESH
    )


def kernel(
    emb_hbm, sign_ref, order_hbm, ct_hbm, out_ref, new_ref,
    emb_ref, order_ref, ct_ref, wide, send, x_ref,
    part, part_rows, energy_ref, got_dims, got_rows,
    c_ref, cb_ref, caug_ref, rt_ref, own_ref, dt_ref, sums_ref,
    t_0, t_1, e_0, e_1, e_2, e_3, left_0, left_1, top_0, top_1,
    low, counts, got_low, got_counts, both, got_both, all_ref,
    load_sem, emb_sem, send_sem, recv_sem, esend_dims, erecv_dims, esend_rows, erecv_rows,
    sem_a, sem_b, sem_c, sem_d, sem_e, sem_f, sem_g, sem_h, sem_i, sem_j,
):
    r, d = lax.axis_index("rows"), lax.axis_index("dims")
    n_rows, n_dims = lax.axis_size("rows"), lax.axis_size("dims")
    devices, piece, inner = send.shape
    block = emb_ref.shape[0]
    subspaces, width, codes = ct_ref.shape
    outer, all_rows, _ = x_ref.shape
    rows = rt_ref.shape[1]
    blocks = all_rows // rows
    per_block = rows // piece
    group = subspaces // n_dims
    half = codes * group // n_rows
    halves = codes // half
    chunks = emb_sem.shape[0]
    chunk = block // chunks

    order_load = pltpu.make_async_copy(order_hbm, order_ref, load_sem.at[0])
    ct_load = pltpu.make_async_copy(ct_hbm, ct_ref, load_sem.at[1])

    def emb_load(i):
        at = pl.ds(pl.multiple_of(i * chunk, chunk), chunk)
        return pltpu.make_async_copy(emb_hbm.at[at], emb_ref.at[at], emb_sem.at[i])

    for i in range(chunks):
        emb_load(i).start()
    order_load.start()
    ct_load.start()

    barrier = pltpu.get_barrier_semaphore()

    to_dims = [lax.rem(d + k, n_dims) for k in range(n_dims)]
    to_zs = [lax.rem(r // SIDE + i, SIDE) * SIDE for i in range(SIDE)]
    to_xs = [lax.rem(r + i, SIDE) for i in range(SIDE)]

    def hops(step):
        return sum(min(i, SIDE - i) for i in (step[0], step[1], step[2] // 2))

    steps = [(i, j, k) for i in range(SIDE) for j in range(SIDE) for k in range(n_dims)]
    for i, j, k in sorted(steps, key=hops, reverse=True):
        if i or j or k:
            pl.semaphore_signal(barrier, inc=1, device_id=(to_zs[i] + to_xs[j], to_dims[k]), device_id_type=MESH)

    sign = sign_ref[...].astype(F32)

    def widen(i, acc):
        emb_load(i).wait()
        step = 256
        for h in range(chunk // step):
            at = pl.ds(pl.multiple_of(i * chunk + h * step, step), step)
            v = emb_ref[at, :].astype(F32)
            wide[at, :] = v * sign
            acc = acc + jnp.sum((v * v).reshape(step // 8, 8, inner), axis=0)
        return acc

    part[...] = lax.fori_loop(0, chunks, widen, jnp.zeros((8, inner), F32))
    order_load.wait()

    def target(s, i, k):
        to_r = to_zs[i] + lax.rem(r + s + SIDE - i, SIDE)
        if isinstance(k, int):
            return to_r, to_dims[(k + 2 * i) % n_dims]
        return to_r, lax.rem(d + k + 2 * i, n_dims)

    def slot(s, i):
        return pl.ds(pl.multiple_of((s * per_block + i) * piece, piece), piece)

    def gather(s, i, k):
        to_r, to_d = target(s, i, k)
        q = to_r * n_dims + to_d
        first = q * piece
        for v in range(0, piece, 16):
            got = [wide[pl.ds(order_ref[first + v + u], 1), :] for u in range(16)]
            send[q, v : v + 16, :] = jnp.concatenate(got, axis=0).astype(BF16)

    def issue(s, i, k):
        to_r, to_d = target(s, i, k)
        q = to_r * n_dims + to_d
        remote(send.at[q], x_ref.at[d, slot(s, i), :], (to_r, to_d), send_sem.at[s], recv_sem.at[s]).start()

    def gather_block(s):
        def step(k, carry):
            for i in range(per_block):
                gather(s, i, k)
            return carry

        lax.fori_loop(0, n_dims, step, 0)

    def issue_block(s, first, last):
        for n in range(first, last):
            issue(s, n % per_block, n // per_block)

    for b in range(blocks):
        gather_block(b)
    pl.semaphore_wait(barrier, devices - 1)

    for k in range(1, n_dims):
        there = (r, to_dims[k])
        remote(part, got_dims.at[k], there, esend_dims.at[k], erecv_dims.at[k]).start()
    pltpu.make_async_copy(send.at[r * n_dims + d], x_ref.at[d, slot(0, 0), :], recv_sem.at[0]).start()
    issue_block(0, 1, n_dims * per_block)

    total = part[...]
    for k in range(1, n_dims):
        wait_bytes(part, erecv_dims.at[k])
        total = total + got_dims[k]
    part_rows[...] = total
    for k in range(1, n_rows):
        there = (lax.rem(r + k, n_rows), d)
        remote(part_rows, got_rows.at[k], there, esend_rows.at[k], erecv_rows.at[k]).start()
    ct_load.wait()

    def prep(i, carry):
        for k in range(8):
            prepare_codes(i * 8 + k, ct_ref, c_ref, cb_ref, caug_ref)
            sums_ref[i * 8 + k] = jnp.zeros(sums_ref.shape[1:], F32)
        return carry

    lax.fori_loop(0, subspaces // 8, prep, 0)
    wait_bytes(send.at[pl.ds(0, per_block * n_dims - 1)], send_sem.at[0])
    issue_block(1, 0, n_dims * per_block)

    cores = 2
    ys = n_dims // cores
    y, core = d // cores, lax.rem(d, cores)

    def chunk_at(k):
        return lax.rem(y + k // cores, ys) * cores + lax.rem(core + lax.rem(k, cores), cores)

    def group_sums(k):
        there = chunk_at(k)
        at = pl.ds(pl.multiple_of(there * group, group), group)
        to = (r, there)
        return (
            remote(low.at[at], got_low.at[k], to, sem_a.at[k], sem_b.at[k]),
            remote(counts.at[at], got_counts.at[k], to, sem_c.at[k], sem_d.at[k]),
        )

    def send_sums(k):
        for g in range(group):
            m = chunk_at(k) * group + g
            low[m] = sums_ref[m, 0:width, :].astype(BF16)
            counts[pl.ds(m, 1), :] = sums_ref[m, width : width + 1, :]
        for copy in group_sums(k):
            copy.start()

    def turn(span, h):
        dy = jnp.where(span == 0, 2, jnp.where(span == spans - 1, 0, 1 + 2 * h))
        dcore = jnp.where(span == 0, h, jnp.where(span == spans - 1, 1 - h, span - 1))
        return dy * cores + dcore

    t_refs, e_refs = (t_0, t_1), (e_0, e_1, e_2, e_3)
    left_refs, top_refs = (left_0, left_1), (top_0, top_1)
    spans = subspaces // SPAN

    def flip(s):
        eye = identity(rows)
        for b in range(outer):
            lanes = slice(b * inner, (b + 1) * inner)
            flipped = lax.dot_general(eye, dt_ref[lanes, :], NT, preferred_element_type=F32).astype(BF16)
            for i in range(per_block):
                from_z = lax.rem(r // SIDE + SIDE - i, SIDE)
                from_x = lax.rem(r + 2 * SIDE - s + i, SIDE)
                at = pl.ds(pl.multiple_of((from_z * SIDE + from_x) * piece, piece), piece)
                out_ref[at, lanes] = flipped[i * piece : (i + 1) * piece]

    def one_block(s, carry):
        wait_bytes(x_ref.at[:, pl.ds(pl.multiple_of(s * rows, rows), rows), :], recv_sem.at[s])
        norms = rotate_block(s, rows, x_ref, rt_ref, own_ref, width)

        @pl.when(s == 0)
        def _():
            total = part_rows[...]
            for k in range(1, n_rows):
                wait_bytes(part, erecv_rows.at[k])
                total = total + got_rows[k]
            energy_ref[...] = jnp.broadcast_to(jnp.sum(total, keepdims=True) / (block * n_rows), energy_ref.shape)

        stretch = ANISO_GAIN * subspaces * energy_ref[0:1, 0:1] / (norms * norms + STABILITY_FLOOR)

        def at_step(span, k):
            ahead, k = k // SPAN, k % SPAN
            return chunk_at(turn(lax.rem(span + ahead + spans, spans), k // group)) * group + k % group

        def start(span, k):
            score(at_step(span, k), k, rows, stretch, own_ref, rt_ref, c_ref, cb_ref, t_refs, top_refs)

        def drain(span):
            last = at_step(span, SPAN - 1)
            decode(last, SPAN - 1, rt_ref, caug_ref, dt_ref, e_refs, left_refs)
            accumulate(last - 1, SPAN - 2, sums_ref, e_refs, left_refs)
            accumulate(last, SPAN - 1, sums_ref, e_refs, left_refs)

        def one_span(span, carry):
            for k in range(SPAN):
                start(span, k + 1)
                decode(at_step(span, k - 1), k - 1, rt_ref, caug_ref, dt_ref, e_refs, left_refs)
                m = at_step(span, k - 2)
                if k < 2:
                    m = jnp.where(jnp.logical_or(span == 0, s == blocks - 1), subspaces, m)
                accumulate(m, k - 2, sums_ref, e_refs, left_refs)
                raise_scores(k, t_refs, top_refs, e_refs)

            for late in range(2, blocks):
                for half_block in range(2):

                    @pl.when(jnp.logical_and(s == 0, span == (late - 2) * 2 + half_block))
                    def _():
                        count = n_dims * per_block // 2
                        issue_block(late, half_block * count, (half_block + 1) * count)

            @pl.when(s == blocks - 1)
            def _():
                drain(span)

                @pl.when(span < spans - 1)
                def _():
                    for h in range(SPAN // group):
                        send_sums(turn(span, h))

            return carry

        start(0, 0)
        lax.fori_loop(0, spans, one_span, 0)

        @pl.when(s < blocks - 1)
        def _():
            drain(spans - 1)
            flip(s)

        return carry

    lax.fori_loop(0, blocks, one_block, 0)
    for k in range(1, cores):
        send_sums(k)

    sent = []

    def go(*args):
        copy = remote(*args)
        copy.start()
        sent.append(copy)

    mine = pl.ds(pl.multiple_of(d * group, group), group)
    total = sums_ref[mine, 0:width, :]
    total_counts = sums_ref[mine, width, :]
    for k in range(1, n_dims):
        wait_bytes(got_low.at[k], sem_b.at[k])
        wait_bytes(got_counts.at[k], sem_d.at[k])
        total = total + got_low[k].astype(F32)
        total_counts = total_counts + got_counts[k]
    for g in range(group):
        for h in range(halves):
            lanes = slice(h * half, (h + 1) * half)
            both[g * halves + h, 0:width, :] = total[g, :, lanes]
            both[g * halves + h, width : width + 8, :] = jnp.broadcast_to(total_counts[g : g + 1, lanes], (8, half))
    for k in range(1, n_rows):
        there = lax.rem(r + k, n_rows)
        go(both.at[there], got_both.at[k], (there, d), sem_e.at[k], sem_f.at[k])
    flip(blocks - 1)
    total = both[r]
    for k in range(1, n_rows):
        wait_bytes(got_both.at[k], sem_f.at[k])
        total = total + got_both[k]

    own_g = d * group + r // halves
    own_lanes = pl.ds(pl.multiple_of(lax.rem(r, halves) * half, half), half)
    new = (total[0:width] + PRIOR_MASS * ct_ref[own_g, :, own_lanes].astype(F32)) / (
        total[width : width + 1] + PRIOR_MASS
    )
    all_ref[d, r] = new.astype(BF16)
    for k in range(1, n_rows):
        there = lax.rem(r + k, n_rows)
        go(all_ref.at[d, r], all_ref.at[d, r], (there, d), sem_g.at[k], sem_h.at[k])
    for k in range(1, n_rows):
        wait_bytes(all_ref.at[d, lax.rem(r + n_rows - k, n_rows)], sem_h.at[k])
    partner = (r, y * cores + 1 - core)
    for k in (2, 1, 3):
        go(all_ref.at[d], all_ref.at[d], (r, lax.rem(y + k, ys) * cores + core), sem_i.at[k], sem_j.at[k])
    go(all_ref.at[d], all_ref.at[d], partner, sem_i.at[ys], sem_j.at[ys])

    def publish(e):
        for g in range(group):
            for h in range(halves):
                new_ref[e * group + g, :, h * half : (h + 1) * half] = all_ref[e, g * halves + h].astype(F32)

    publish(d)
    for k in (1, 3, 2):
        e = lax.rem(y + ys - k, ys) * cores + core
        wait_bytes(all_ref.at[e], sem_j.at[k])
        go(all_ref.at[e], all_ref.at[e], partner, sem_i.at[ys + k], sem_j.at[ys + k])
        if k != 2:
            publish(e)
    for k in (0, 1, 3, 2):
        e = lax.rem(y + ys - k, ys) * cores + 1 - core
        if k == 0:
            publish(lax.rem(y + ys - 2, ys) * cores + core)
        wait_bytes(all_ref.at[e], sem_j.at[ys + k])
        publish(e)

    for copy in sent:
        copy.wait_send()
    for k in range(1, n_dims):
        for copy in group_sums(k):
            copy.wait_send()
        wait_bytes(part, esend_dims.at[k])
    for k in range(1, n_rows):
        wait_bytes(part, esend_rows.at[k])
    for s in range(1, blocks):
        wait_bytes(send.at[pl.ds(0, per_block * n_dims)], send_sem.at[s])


def body(embeddings, sign_flips, row_order, codebook):
    ct = codebook.transpose(0, 2, 1)
    n_rows, n_dims = lax.axis_size("rows"), lax.axis_size("dims")
    block, inner = embeddings.shape
    devices = n_rows * n_dims
    piece = block // devices
    subspaces, width, codes = ct.shape
    all_rows = block // n_dims
    rows = 256
    blocks = all_rows // rows
    group = subspaces // n_dims
    half = codes * group // n_rows
    full = n_dims * inner
    vmem = pl.BlockSpec(memory_space=pltpu.VMEM)
    hbm = pl.BlockSpec(memory_space=pl.ANY)
    dma = pltpu.SemaphoreType.DMA
    decoded, new = pl.pallas_call(
        kernel,
        out_shape=(
            pltpu.VMEM((all_rows, full), BF16),
            pltpu.VMEM((subspaces, width, codes), F32),
        ),
        in_specs=[hbm, vmem, hbm, hbm],
        out_specs=(vmem, vmem),
        scratch_shapes=[
            pltpu.VMEM((block, inner), BF16),
            pltpu.SMEM((block,), jnp.int32),
            pltpu.VMEM((subspaces, width, codes), BF16),
            pltpu.VMEM((block, inner), F32),
            pltpu.VMEM((devices, piece, inner), BF16),
            pltpu.VMEM((n_dims, all_rows, inner), BF16),
            pltpu.VMEM((8, inner), F32),
            pltpu.VMEM((8, inner), F32),
            pltpu.VMEM((8, inner), F32),
            pltpu.VMEM((n_dims, 8, inner), F32),
            pltpu.VMEM((n_rows, 8, inner), F32),
            pltpu.VMEM((subspaces, codes, width), BF16),
            pltpu.VMEM((subspaces, codes, LANES), F32),
            pltpu.VMEM((subspaces, 2 * width, codes), BF16),
            pltpu.VMEM((full, rows), BF16),
            pltpu.VMEM((subspaces, rows), F32),
            pltpu.VMEM((full, rows), BF16),
            pltpu.VMEM((subspaces + 1, width + 8, codes), F32),
        ]
        + [pltpu.VMEM((codes, rows), F32)] * 2
        + [pltpu.VMEM((codes, rows), BF16)] * 4
        + [pltpu.VMEM((2 * width, rows), BF16)] * 2
        + [pltpu.VMEM((8, rows), F32)] * 2
        + [
            pltpu.VMEM((subspaces, width, codes), BF16),
            pltpu.VMEM((subspaces, codes), F32),
            pltpu.VMEM((n_dims, group, width, codes), BF16),
            pltpu.VMEM((n_dims, group, codes), F32),
            pltpu.VMEM((n_rows, width + 8, half), F32),
            pltpu.VMEM((n_rows, width + 8, half), F32),
            pltpu.VMEM((n_dims, n_rows, width, half), BF16),
            dma((2,)),
            dma((8,)),
            dma((blocks,)),
            dma((blocks,)),
        ]
        + [dma((n_dims,))] * 2
        + [dma((n_rows,))] * 2
        + [dma((n_dims,))] * 4
        + [dma((n_rows,))] * 4
        + [dma((n_dims,))] * 2,
        compiler_params=pltpu.CompilerParams(
            collective_id=0, has_side_effects=True, vmem_limit_bytes=56 * 1024 * 1024
        ),
        name="update_codes",
    )(embeddings, sign_flips.reshape(1, inner), row_order, ct)
    return decoded, new.transpose(0, 2, 1)


def solution(mesh):
    return jax.shard_map(
        body,
        mesh=mesh,
        in_specs=(P("rows", "dims"), P("dims"), P("rows"), P()),
        out_specs=(P(("rows", "dims"), None), P()),
        check_vma=False,
    )
```
